128 devices in a mesh: narrow: 8 (over y, core), wide: 16 (over x, z).
Axes of the slice: x: 4, y: 4, z: 4, core: 2. Of those that a mesh axis runs over, the one named last changes fastest.
Arguments:
- velocity: float32 [3, 256, 512, 1024], P(None, 'wide', 'narrow'), may hold values from -6 to 6
- exponents: int32 [7], replicated, may hold values from -1 to 2
Outputs:
- approx: float32 [3, 128, 256, 512], P(None, None, 'narrow', 'wide')
- details: float32 [3, 7, 128, 256, 512], P(None, None, 'wide', 'narrow')
The draws below stay inside these ranges and needn't reach their ends.
All inputs are finite; a program needn't handle non-finite values.
Results may differ from the reference program's by a relative error of at most 0.000082.
Values sent between devices are 32-bit elements; how exact they have to be, the bound alone decides.
A program may use at most 256 MiB of HBM per device.

```python
import jax
import jax.numpy as jnp
from jax import lax

NZ = 1024
NX = 256
NY = 512


def set_ends(values, stream_key, smallest, high):
    dims = values.shape
    index_at = [jax.random.randint(jax.random.fold_in(stream_key, axis), (), 0, dims[axis]) for axis in range(len(dims))]
    values = values.at[tuple(index_at)].set(smallest)
    longest = dims.index(max(dims))
    index_at[longest] = (index_at[longest] + 1) % dims[longest]
    return values.at[tuple(index_at)].set(high)


def steps_of(stream_key, shape, cuts, least, high):
    level = 1.0
    for axis_at, shards_of in cuts:
        steps = jax.random.uniform(jax.random.fold_in(jax.random.fold_in(stream_key, 6), axis_at), (shards_of,), jnp.float32, least / len(cuts), high / len(cuts))
        level = level * jnp.repeat(jnp.exp(steps), shape[axis_at] // shards_of).reshape((-1,) + (1,) * (len(shape) - 1 - axis_at))
    return level


def centred(stream_key, dims, spread, most, shards=(), dtype=jnp.bfloat16):
    array = jax.random.normal(stream_key, dims, jnp.float32) * spread
    if len(shards) > 0:
        array = steps_of(stream_key, dims, shards, -0.22, 0.18) * array
    return jnp.clip(array, min=-most, max=most).astype(dtype)


def setup_inputs(seed: int = 0) -> dict:
    keys = jax.random.split(jax.random.key(seed), 3)
    return {
        "velocity": centred(keys[0], (3, NX, NY, NZ), 1.0, 6.0, ((1, 16), (2, 8)), jnp.float32),
        "exponents": set_ends(jax.random.randint(keys[1], (7,), -1, 3), jax.random.fold_in(keys[1], 1), -1, 2).astype(jnp.int32),
    }


predict_one = -1.586134342
update_one = -0.05298011854
predict_two = 0.8829110762
update_two = 0.4435068522
scaling = 1.149604398
inverse_scaling = 1.0 / 1.149604398


def cut_range(block_data, begin_at, end_at, dimension):
    return lax.slice_in_dim(block_data, begin_at, end_at, 1, dimension)


def lift_extended(extended, dimension):
    length = extended.shape[dimension]
    pair_count = length // 2
    even_part = lax.slice_in_dim(extended, 0, length, 2, dimension)
    odd_part = lax.slice_in_dim(extended, 1, length, 2, dimension)
    odd_part = cut_range(odd_part, 0, pair_count - 1, dimension) + predict_one * (
        cut_range(even_part, 0, pair_count - 1, dimension) + cut_range(even_part, 1, pair_count, dimension))
    even_part = cut_range(even_part, 1, pair_count - 1, dimension) + update_one * (
        cut_range(odd_part, 0, pair_count - 2, dimension) + cut_range(odd_part, 1, pair_count - 1, dimension))
    odd_part = cut_range(odd_part, 1, pair_count - 2, dimension) + predict_two * (
        cut_range(even_part, 0, pair_count - 3, dimension) + cut_range(even_part, 1, pair_count - 2, dimension))
    even_part = cut_range(even_part, 1, pair_count - 3, dimension) + update_two * (
        cut_range(odd_part, 0, pair_count - 4, dimension) + cut_range(odd_part, 1, pair_count - 3, dimension))
    return even_part * scaling, cut_range(odd_part, 1, pair_count - 3, dimension) * inverse_scaling


def lift_axis(block_data, dimension):
    widths = [(0, 0)] * block_data.ndim
    widths[dimension] = (4, 4)
    return lift_extended(jnp.pad(block_data, widths, mode="reflect"), dimension)


def transform_component(component):
    subbands = []
    for along_x in lift_axis(component, 0):
        for along_y in lift_axis(along_x, 1):
            for along_z in lift_axis(along_y, 2):
                subbands.append(along_z)
    return subbands[0], jnp.stack(subbands[1:])


def reference(velocity, exponents):
    approx, details = lax.map(transform_component, velocity)
    step_sizes = jnp.exp2(exponents.astype(jnp.float32))
    scaled = details / step_sizes[None, :, None, None, None]
    return approx, scaled - jnp.clip(scaled, -0.5, 0.5)
```

```python
import functools

import jax
import jax.numpy as jnp
import ml_dtypes
import numpy as np
from jax import lax
from jax.experimental import pallas as pl
from jax.experimental.pallas import tpu as pltpu
from jax.sharding import PartitionSpec as P

MESH = pl.DeviceIdType.MESH
F32 = jnp.float32
BF16 = jnp.bfloat16

pa = -1.586134342
ub = -0.05298011854
pg = 0.8829110762
ue = 0.4435068522
scaling = 1.149604398

COMPS = 3
PLANES = 16
ROWS = 64
DEPTH = 1024
CHUNKS = DEPTH // 128
TILE = 256
WINDOW_START = (0, 128, 384, 512)
WINDOW_KIND = (0, 1, 1, 2)


def z_weights():
    ext = np.pad(np.eye(DEPTH), ((0, 0), (4, 4)), mode="reflect")
    s, d = ext[:, 0::2], ext[:, 1::2]
    d = d[:, :-1] + pa * (s[:, :-1] + s[:, 1:])
    s = s[:, 1:-1] + ub * (d[:, :-1] + d[:, 1:])
    d = d[:, 1:-1] + pg * (s[:, :-1] + s[:, 1:])
    s = s[:, 1:-1] + ue * (d[:, :-1] + d[:, 1:])
    low, high = s * scaling, d[:, 1:] / scaling
    kinds = []
    for k in (0, 1, 3):
        rows = slice(WINDOW_START[k], WINDOW_START[k] + 512)
        cols = slice(128 * k, 128 * k + 128)
        kinds.append(np.concatenate([low[rows, cols], high[rows, cols]], 1))
    full = np.stack(kinds)
    head = full.astype(np.float32).astype(ml_dtypes.bfloat16)
    rest = (full - head.astype(np.float64)).astype(np.float32).astype(ml_dtypes.bfloat16)
    return np.stack([head, rest], 1)


def kernel(
    n_narrow, n_wide,
    x_ref, e_ref, w_ref, ap_ref, det_ref,
    a_buf, b_buf, hl, wv, ys, yr, yz, xs, xr, lll, lsend, lrecv,
    load_sem, w_sem, y_send, y_recv, x_send, x_recv, l_send, l_recv,
):
    nar = lax.axis_index("narrow")
    wid = lax.axis_index("wide")
    up = lax.rem(nar + n_narrow - 1, n_narrow)
    down = lax.rem(nar + 1, n_narrow)
    left = lax.rem(wid + n_wide - 1, n_wide)
    right = lax.rem(wid + 1, n_wide)
    has_up, has_down = nar > 0, nar < n_narrow - 1
    has_left, has_right = wid > 0, wid < n_wide - 1

    def load(c, j):
        return pltpu.make_async_copy(
            x_ref.at[c, :, pl.ds(128 * j, 128)], a_buf.at[c, j], load_sem.at[c, j]
        )

    load_w = pltpu.make_async_copy(w_ref, wv, w_sem)
    for j in range(CHUNKS):
        load(0, j).start()
    load_w.start()
    for c in range(1, COMPS):
        for j in range(CHUNKS):
            load(c, j).start()

    barrier = pltpu.get_barrier_semaphore()

    def greet(off, carry):
        pl.semaphore_signal(
            barrier, inc=1, device_id={"wide": lax.rem(wid + off, n_wide)}, device_id_type=MESH
        )
        return carry

    lax.fori_loop(1, n_wide, greet, 0)

    @pl.when(has_up)
    def _():
        pl.semaphore_signal(barrier, inc=1, device_id={"narrow": up}, device_id_type=MESH)

    @pl.when(has_down)
    def _():
        pl.semaphore_signal(barrier, inc=1, device_id={"narrow": down}, device_id_type=MESH)

    pl.semaphore_wait(
        barrier, n_wide - 1 + has_up.astype(jnp.int32) + has_down.astype(jnp.int32)
    )

    def y_copy(side, c):
        return pltpu.make_async_remote_copy(
            src_ref=ys.at[side, c],
            dst_ref=yr.at[1 - side, c],
            send_sem=y_send.at[side, c],
            recv_sem=y_recv.at[1 - side, c],
            device_id={"narrow": up if side == 0 else down},
            device_id_type=MESH,
        )

    def y_values(c):
        for j in range(CHUNKS):
            load(c, j).wait()

        def body(j, carry):
            def row(r):
                return a_buf[c, j, pl.ds(r, PLANES, stride=ROWS), :]

            r0, r1, r2 = row(0), row(1), row(2)
            e0, e1, e2, e3 = row(ROWS - 4), row(ROWS - 3), row(ROWS - 2), row(ROWS - 1)
            before_last = e1 + pa * (e0 + e2)
            ys[0, c, j, 0:PLANES, :] = r0
            ys[0, c, j, PLANES:, :] = r1 + pa * (r0 + r2)
            ys[1, c, j, 0:PLANES, :] = e3 + pa * e2
            ys[1, c, j, PLANES:, :] = e2 + ub * before_last

            @pl.when(jnp.logical_not(has_up))
            def _():
                r3, r4 = row(3), row(4)
                yr[0, c, j, 0:PLANES, :] = r1 + pa * r2
                yr[0, c, j, PLANES:, :] = r2 + ub * (r3 + pa * (r2 + r4))

            @pl.when(jnp.logical_not(has_down))
            def _():
                yr[1, c, j, 0:PLANES, :] = e2
                yr[1, c, j, PLANES:, :] = before_last

            return carry

        lax.fori_loop(0, CHUNKS, body, 0)

        @pl.when(has_up)
        def _():
            y_copy(0, c).start()

        @pl.when(has_down)
        def _():
            y_copy(1, c).start()

    def z_rows(m, get, put):
        for j in range(CHUNKS):
            value = get(j)
            head = value.astype(BF16)
            hl[0:m, 128 * j : 128 * j + 128] = head
            hl[m : 2 * m, 128 * j : 128 * j + 128] = (value - head.astype(F32)).astype(BF16)
        for k in range(CHUNKS // 2):
            start, kind = WINDOW_START[k], WINDOW_KIND[k]
            both = jnp.dot(
                hl[0 : 2 * m, start : start + 512], wv[kind, 0], preferred_element_type=F32
            )
            rest = jnp.dot(hl[0:m, start : start + 512], wv[kind, 1], preferred_element_type=F32)
            out = both[:m] + (both[m:] + rest)
            put(k, out[:, :128])
            put(CHUNKS // 2 + k, out[:, 128:])

    def z_tiles(c, first, step):
        def body(t, carry):
            base = pl.multiple_of((first + step * t) * TILE, TILE)

            def put(j, value):
                b_buf[c, j, pl.ds(base, TILE), :] = value

            z_rows(TILE, lambda j: a_buf[c, j, pl.ds(base, TILE), :], put)
            return carry

        lax.fori_loop(0, 2, body, 0)

    def z_halo(c):
        @pl.when(has_up)
        def _():
            y_copy(1, c).wait_recv()

        @pl.when(has_down)
        def _():
            y_copy(0, c).wait_recv()

        def put(j, value):
            yz[c, j] = value

        z_rows(
            4 * PLANES,
            lambda j: jnp.concatenate([yr[0, c, j], yr[1, c, j]], 0),
            put,
        )

    half = ROWS // 2
    row_at = lax.broadcasted_iota(jnp.int32, (half, 128), 0)

    def following(value, last):
        return jnp.where(row_at == half - 1, last, pltpu.roll(value, half - 1, 0))

    def preceding(value, first):
        return jnp.where(row_at == 0, first, pltpu.roll(value, 1, 0))

    def y_plane(c, p, j):
        base = pl.multiple_of(p * ROWS, ROWS)
        s = b_buf[c, j, pl.ds(base, half, stride=2), :]
        d = b_buf[c, j, pl.ds(base + 1, half, stride=2), :]
        pv = yz[c, j, pl.ds(p, 1), :]
        qv = yz[c, j, pl.ds(PLANES + p, 1), :]
        sv = yz[c, j, pl.ds(2 * PLANES + p, 1), :]
        dv = yz[c, j, pl.ds(3 * PLANES + p, 1), :]
        d = d + pa * (s + following(s, sv))
        dm = pv + pa * s[0:1]
        s = s + ub * (preceding(d, dm) + d)
        sn = sv + ub * (d[half - 1 :] + dv)
        sm = qv + ub * dm
        dm = dm + pg * (sm + s[0:1])
        d = d + pg * (s + following(s, sn))
        s = s + ue * (preceding(d, dm) + d)
        a_buf[c, j, pl.ds(base, half), :] = s
        a_buf[c, j, pl.ds(base + half, half), :] = d

    def y_planes(c, starts):
        for start in starts:
            def body(q, carry):
                for j in range(CHUNKS):
                    y_plane(c, start + q, j)
                return carry

            lax.fori_loop(0, 4, body, 0)

    parts = ((0, 4, 0, half), (4, 4, 0, half), (0, 8, half, half))

    def x_copy(side, c, part):
        j0, jn, r0, rn = parts[part]
        place = (c, slice(None), pl.ds(j0, jn), pl.ds(r0, rn), slice(None))
        return pltpu.make_async_remote_copy(
            src_ref=xs.at[(side, *place)],
            dst_ref=xr.at[(1 - side, *place)],
            send_sem=x_send.at[side, c, part],
            recv_sem=x_recv.at[1 - side, c, part],
            device_id={"wide": left if side == 0 else right},
            device_id_type=MESH,
        )

    def x_values(c):
        def body(j, carry):
            def plane(p):
                return a_buf[c, j, p * ROWS : p * ROWS + ROWS, :]

            p0 = plane(0)
            xs[0, c, 0, j] = p0
            xs[0, c, 1, j] = plane(1) + pa * (p0 + plane(2))
            e2 = plane(PLANES - 2)
            xs[1, c, 0, j] = plane(PLANES - 1) + pa * e2
            xs[1, c, 1, j] = e2 + ub * (plane(PLANES - 3) + pa * (plane(PLANES - 4) + e2))
            return carry

        lax.fori_loop(0, CHUNKS, body, 0)

    def x_ends():
        def body(at, carry):
            c, j = at // CHUNKS, lax.rem(at, CHUNKS)

            def plane(p):
                return a_buf[c, j, p * ROWS : p * ROWS + ROWS, :]

            @pl.when(jnp.logical_not(has_left))
            def _():
                xr[0, c, 0, j] = plane(1) + pa * plane(2)
                xr[0, c, 1, j] = plane(2) + ub * (plane(3) + pa * (plane(2) + plane(4)))

            @pl.when(jnp.logical_not(has_right))
            def _():
                xr[1, c, 0, j] = plane(PLANES - 2)
                xr[1, c, 1, j] = plane(PLANES - 3) + pa * (plane(PLANES - 4) + plane(PLANES - 2))

            return carry

        lax.fori_loop(0, COMPS * CHUNKS, body, 0)

    def x_start(c, part):
        @pl.when(has_left)
        def _():
            x_copy(0, c, part).start()

        @pl.when(has_right)
        def _():
            x_copy(1, c, part).start()

    def x_arrived(c, part):
        @pl.when(has_left)
        def _():
            x_copy(1, c, part).wait_recv()

        @pl.when(has_right)
        def _():
            x_copy(0, c, part).wait_recv()

    def factor(band):
        shift = lax.shift_left(jnp.int32(1), 15 - e_ref[band - 1]).astype(F32)
        ups = 2 - 2 * (band // 4) - 2 * ((band // 2) % 2)
        return shift * (2.0**-15 * scaling**ups)

    def x_lift(c, by, bz):
        low_band, high_band = 2 * by + bz, 4 + 2 * by + bz
        high_scale = factor(high_band)
        low_scale = factor(low_band) if low_band else None

        def body(at, carry):
            k, t = at // 4, lax.rem(at, 4)
            j = 4 * bz + k
            row = pl.multiple_of(half * by + 8 * t, 8)

            def plane(p):
                return a_buf[c, j, pl.ds(pl.multiple_of(p * ROWS + row, 8), 8), :]

            s = [plane(2 * i) for i in range(8)]
            d = [plane(2 * i + 1) for i in range(8)]
            pv = xr[0, c, 0, j, pl.ds(row, 8), :]
            qv = xr[0, c, 1, j, pl.ds(row, 8), :]
            sv = xr[1, c, 0, j, pl.ds(row, 8), :]
            dv = xr[1, c, 1, j, pl.ds(row, 8), :]
            s.append(sv)
            d = [d[i] + pa * (s[i] + s[i + 1]) for i in range(8)]
            dm = pv + pa * s[0]
            sn = sv + ub * (d[7] + dv)
            sm = qv + ub * dm
            s = [s[i] + ub * ((d[i - 1] if i else dm) + d[i]) for i in range(8)]
            dm = dm + pg * (sm + s[0])
            s.append(sn)
            d = [d[i] + pg * (s[i] + s[i + 1]) for i in range(8)]
            s = [s[i] + ue * ((d[i - 1] if i else dm) + d[i]) for i in range(8)]
            lanes = pl.ds(pl.multiple_of(128 * k, 128), 128)
            rows = pl.ds(pl.multiple_of(8 * t, 8), 8)
            for i in range(8):
                v = d[i] * high_scale
                det_ref[c, high_band - 1, i, rows, lanes] = v - jnp.clip(v, -0.5, 0.5)
                if low_band:
                    v = s[i] * low_scale
                    det_ref[c, low_band - 1, i, rows, lanes] = v - jnp.clip(v, -0.5, 0.5)
                else:
                    lll[k, pl.ds(pl.multiple_of(half * i + 8 * t, 8), 8), :] = s[i] * (scaling * scaling)
            return carry

        lax.fori_loop(0, 16, body, 0)

    lane = lax.broadcasted_iota(jnp.int32, (8, 128), 1)
    low_half = lane < 64
    low_quarter = lax.rem(lane, 64) < 32

    def l_copy(c, peer, source):
        return pltpu.make_async_remote_copy(
            src_ref=lsend.at[peer, c],
            dst_ref=lrecv.at[c, :, pl.ds(pl.multiple_of(source * 8, 8), 8), :],
            send_sem=l_send.at[c, peer],
            recv_sem=l_recv.at[c, source],
            device_id={"wide": peer},
            device_id_type=MESH,
        )

    def l_pack(c):
        def body(at, carry):
            k, g = at // 8, lax.rem(at, 8)
            v = [lll[k, pl.ds(4 * g + y, 8, stride=half), :] for y in range(4)]
            for a, b in ((0, 2), (1, 3)):
                v[a], v[b] = (
                    jnp.where(low_half, v[a], pltpu.roll(v[b], 64, 1)),
                    jnp.where(low_half, pltpu.roll(v[a], 64, 1), v[b]),
                )
            for a, b in ((0, 1), (2, 3)):
                v[a], v[b] = (
                    jnp.where(low_quarter, v[a], pltpu.roll(v[b], 32, 1)),
                    jnp.where(low_quarter, pltpu.roll(v[a], 96, 1), v[b]),
                )
            for y in range(4):
                lsend[4 * k + y, c, g] = v[y]
            return carry

        lax.fori_loop(0, 32, body, 0)

        def send(off, carry):
            l_copy(c, lax.rem(wid + off, n_wide), wid).start()
            return carry

        lax.fori_loop(1, n_wide, send, 0)
        lrecv[c, :, pl.ds(pl.multiple_of(wid * 8, 8), 8), :] = lsend[wid, c]

    def l_take(c):
        def arrived(off, carry):
            source = lax.rem(wid + off, n_wide)
            l_copy(c, source, source).wait_recv()
            return carry

        lax.fori_loop(1, n_wide, arrived, 0)

        def body(g, carry):
            ap_ref[c, pl.ds(pl.multiple_of(128 * g, 128), 128), :] = lrecv[c, g].T
            return carry

        lax.fori_loop(0, 8, body, 0)

    y_values(0)
    load_w.wait()
    z_tiles(0, 0, 3)
    y_values(1)
    y_values(2)
    for c in range(COMPS):
        if c:
            z_tiles(c, 0, 3)
        z_halo(c)
        y_planes(c, (0, 12))
        x_values(c)
        x_start(c, 0)
        x_start(c, 1)
    for c in range(COMPS):
        x_start(c, 2)
    for c in range(COMPS):
        z_tiles(c, 1, 1)
        y_planes(c, (4, 8))
    x_ends()
    for c in range(COMPS):
        x_arrived(c, 0)
        x_lift(c, 0, 0)
        l_pack(c)
        x_arrived(c, 1)
        x_lift(c, 0, 1)
    for c in range(COMPS):
        x_arrived(c, 2)
        x_lift(c, 1, 0)
        x_lift(c, 1, 1)
        l_take(c)

    for c in range(COMPS):
        @pl.when(has_up)
        def _():
            y_copy(0, c).wait_send()

        @pl.when(has_down)
        def _():
            y_copy(1, c).wait_send()

        for part in range(3):
            @pl.when(has_left)
            def _():
                x_copy(0, c, part).wait_send()

            @pl.when(has_right)
            def _():
                x_copy(1, c, part).wait_send()

        def sent(off, carry):
            peer = lax.rem(wid + off, n_wide)
            l_copy(c, peer, wid).wait_send()
            return carry

        lax.fori_loop(1, n_wide, sent, 0)


def local(n_narrow, n_wide, velocity, exponents):
    cells = velocity.reshape((COMPS, PLANES * ROWS, DEPTH))
    approx, details = pl.pallas_call(
        functools.partial(kernel, n_narrow, n_wide),
        out_shape=(
            jax.ShapeDtypeStruct((COMPS, 1024, 128), F32),
            jax.ShapeDtypeStruct((COMPS, 7, PLANES // 2, ROWS // 2, DEPTH // 2), F32),
        ),
        in_specs=[
            pl.BlockSpec(memory_space=pl.ANY),
            pl.BlockSpec(memory_space=pltpu.SMEM),
            pl.BlockSpec(memory_space=pl.ANY),
        ],
        out_specs=(
            pl.BlockSpec(memory_space=pltpu.VMEM),
            pl.BlockSpec(memory_space=pltpu.VMEM),
        ),
        scratch_shapes=[
            pltpu.VMEM((COMPS, CHUNKS, PLANES * ROWS, 128), F32),
            pltpu.VMEM((COMPS, CHUNKS, PLANES * ROWS, 128), F32),
            pltpu.VMEM((2 * TILE, DEPTH), BF16),
            pltpu.VMEM((3, 2, 512, 256), BF16),
            pltpu.VMEM((2, COMPS, CHUNKS, 2 * PLANES, 128), F32),
            pltpu.VMEM((2, COMPS, CHUNKS, 2 * PLANES, 128), F32),
            pltpu.VMEM((COMPS, CHUNKS, 4 * PLANES, 128), F32),
            pltpu.VMEM((2, COMPS, 2, CHUNKS, ROWS, 128), F32),
            pltpu.VMEM((2, COMPS, 2, CHUNKS, ROWS, 128), F32),
            pltpu.VMEM((4, 256, 128), F32),
            pltpu.VMEM((16, COMPS, 8, 8, 128), F32),
            pltpu.VMEM((COMPS, 8, 128, 128), F32),
            pltpu.SemaphoreType.DMA((COMPS, CHUNKS)),
            pltpu.SemaphoreType.DMA,
            pltpu.SemaphoreType.DMA((2, COMPS)),
            pltpu.SemaphoreType.DMA((2, COMPS)),
            pltpu.SemaphoreType.DMA((2, COMPS, 3)),
            pltpu.SemaphoreType.DMA((2, COMPS, 3)),
            pltpu.SemaphoreType.DMA((COMPS, 16)),
            pltpu.SemaphoreType.DMA((COMPS, 16)),
        ],
        compiler_params=pltpu.CompilerParams(
            collective_id=0, has_side_effects=True, vmem_limit_bytes=60 * 1024 * 1024
        ),
        cost_estimate=pl.CostEstimate(
            flops=10_000_000_000, bytes_accessed=26_000_000, transcendentals=0
        ),
    )(cells, exponents, jnp.asarray(z_weights()))
    approx = approx.reshape((COMPS, ROWS // 2, 32, 128))
    return jnp.transpose(approx, (0, 3, 1, 2)), details


def solution(mesh):
    placed = (P(None, "wide", "narrow", None), P())
    return jax.shard_map(
        functools.partial(local, mesh.shape["narrow"], mesh.shape["wide"]),
        mesh=mesh,
        in_specs=placed,
        out_specs=(P(None, None, "narrow", "wide"), P(None, None, "wide", "narrow", None)),
        check_vma=False,
    )
```

```python
import functools

import jax
import jax.numpy as jnp
import ml_dtypes
import numpy as np
from jax import lax
from jax.experimental import pallas as pl
from jax.experimental.pallas import tpu as pltpu
from jax.sharding import PartitionSpec as P

MESH = pl.DeviceIdType.MESH
F32 = jnp.float32
BF16 = jnp.bfloat16

pa = -1.586134342
ub = -0.05298011854
pg = 0.8829110762
ue = 0.4435068522
scaling = 1.149604398

COMPS = 3
PLANES = 16
ROWS = 64
DEPTH = 1024
CHUNKS = DEPTH // 128
TILE = 256
WINDOW_START = (0, 128, 384, 512)
WINDOW_KIND = (0, 1, 1, 2)


def z_weights():
    ext = np.pad(np.eye(DEPTH), ((0, 0), (4, 4)), mode="reflect")
    s, d = ext[:, 0::2], ext[:, 1::2]
    d = d[:, :-1] + pa * (s[:, :-1] + s[:, 1:])
    s = s[:, 1:-1] + ub * (d[:, :-1] + d[:, 1:])
    d = d[:, 1:-1] + pg * (s[:, :-1] + s[:, 1:])
    s = s[:, 1:-1] + ue * (d[:, :-1] + d[:, 1:])
    low, high = s * scaling, d[:, 1:] / scaling
    kinds = []
    for k in (0, 1, 3):
        rows = slice(WINDOW_START[k], WINDOW_START[k] + 512)
        cols = slice(128 * k, 128 * k + 128)
        kinds.append(np.concatenate([low[rows, cols], high[rows, cols]], 1))
    full = np.stack(kinds)
    head = full.astype(np.float32).astype(ml_dtypes.bfloat16)
    rest = (full - head.astype(np.float64)).astype(np.float32).astype(ml_dtypes.bfloat16)
    return np.stack([head, rest], 1)


def kernel(
    n_narrow, n_wide,
    x_ref, e_ref, w_ref, ap_ref, det_ref,
    a_buf, b_buf, hl, wv, ys, yr, yz, xs, xr, lll, lsend, lmid, lrecv,
    load_sem, w_sem, y_send, y_recv, x_send, x_recv, l_send, l_recv,
):
    nar = lax.axis_index("narrow")
    wid = lax.axis_index("wide")
    up = lax.rem(nar + n_narrow - 1, n_narrow)
    down = lax.rem(nar + 1, n_narrow)
    left = lax.rem(wid + n_wide - 1, n_wide)
    right = lax.rem(wid + 1, n_wide)
    has_up, has_down = nar > 0, nar < n_narrow - 1
    has_left, has_right = wid > 0, wid < n_wide - 1

    def load(c, j):
        return pltpu.make_async_copy(
            x_ref.at[c, :, pl.ds(128 * j, 128)], a_buf.at[c, j], load_sem.at[c, j]
        )

    load_w = pltpu.make_async_copy(w_ref, wv, w_sem)
    for j in range(CHUNKS):
        load(0, j).start()
    load_w.start()

    barrier = pltpu.get_barrier_semaphore()

    def greet(off, carry):
        pl.semaphore_signal(
            barrier, inc=1, device_id={"wide": lax.rem(wid + off, n_wide)}, device_id_type=MESH
        )
        return carry

    lax.fori_loop(1, n_wide, greet, 0)

    @pl.when(has_up)
    def _():
        pl.semaphore_signal(barrier, inc=1, device_id={"narrow": up}, device_id_type=MESH)

    @pl.when(has_down)
    def _():
        pl.semaphore_signal(barrier, inc=1, device_id={"narrow": down}, device_id_type=MESH)

    pl.semaphore_wait(
        barrier, n_wide - 1 + has_up.astype(jnp.int32) + has_down.astype(jnp.int32)
    )

    def y_copy(side, c):
        return pltpu.make_async_remote_copy(
            src_ref=ys.at[side, c],
            dst_ref=yr.at[1 - side, c],
            send_sem=y_send.at[side, c],
            recv_sem=y_recv.at[1 - side, c],
            device_id={"narrow": up if side == 0 else down},
            device_id_type=MESH,
        )

    def y_values(c):
        for j in range(CHUNKS):
            load(c, j).wait()
        if c + 1 < COMPS:
            for j in range(CHUNKS):
                load(c + 1, j).start()

        def body(j, carry):
            def row(r):
                return a_buf[c, j, pl.ds(r, PLANES, stride=ROWS), :]

            r0, r1, r2 = row(0), row(1), row(2)
            e0, e1, e2, e3 = row(ROWS - 4), row(ROWS - 3), row(ROWS - 2), row(ROWS - 1)
            before_last = e1 + pa * (e0 + e2)
            ys[0, c, j, 0:PLANES, :] = r0
            ys[0, c, j, PLANES:, :] = r1 + pa * (r0 + r2)
            ys[1, c, j, 0:PLANES, :] = e3 + pa * e2
            ys[1, c, j, PLANES:, :] = e2 + ub * before_last

            @pl.when(jnp.logical_not(has_up))
            def _():
                r3, r4 = row(3), row(4)
                yr[0, c, j, 0:PLANES, :] = r1 + pa * r2
                yr[0, c, j, PLANES:, :] = r2 + ub * (r3 + pa * (r2 + r4))

            @pl.when(jnp.logical_not(has_down))
            def _():
                yr[1, c, j, 0:PLANES, :] = e2
                yr[1, c, j, PLANES:, :] = before_last

            return carry

        lax.fori_loop(0, CHUNKS, body, 0)

        @pl.when(has_up)
        def _():
            y_copy(0, c).start()

        @pl.when(has_down)
        def _():
            y_copy(1, c).start()

    def z_rows(m, get, put):
        for j in range(CHUNKS):
            value = get(j)
            head = value.astype(BF16)
            hl[0:m, 128 * j : 128 * j + 128] = head
            hl[m : 2 * m, 128 * j : 128 * j + 128] = (value - head.astype(F32)).astype(BF16)
        for k in range(CHUNKS // 2):
            start, kind = WINDOW_START[k], WINDOW_KIND[k]
            both = jnp.dot(
                hl[0 : 2 * m, start : start + 512], wv[kind, 0], preferred_element_type=F32
            )
            rest = jnp.dot(hl[0:m, start : start + 512], wv[kind, 1], preferred_element_type=F32)
            out = both[:m] + (both[m:] + rest)
            put(k, out[:, :128])
            put(CHUNKS // 2 + k, out[:, 128:])

    def z_tiles(c, first, step):
        def body(t, carry):
            base = pl.multiple_of((first + step * t) * TILE, TILE)

            def put(j, value):
                b_buf[c, j, pl.ds(base, TILE), :] = value

            z_rows(TILE, lambda j: a_buf[c, j, pl.ds(base, TILE), :], put)
            return carry

        lax.fori_loop(0, 2, body, 0)

    def z_halo(c):
        @pl.when(has_up)
        def _():
            y_copy(1, c).wait_recv()

        @pl.when(has_down)
        def _():
            y_copy(0, c).wait_recv()

        def put(j, value):
            yz[c, j] = value

        z_rows(
            4 * PLANES,
            lambda j: jnp.concatenate([yr[0, c, j], yr[1, c, j]], 0),
            put,
        )

    half = ROWS // 2
    row_at = lax.broadcasted_iota(jnp.int32, (half, 128), 0)

    def following(value, last):
        return jnp.where(row_at == half - 1, last, pltpu.roll(value, half - 1, 0))

    def preceding(value, first):
        return jnp.where(row_at == 0, first, pltpu.roll(value, 1, 0))

    def y_plane(c, p, j):
        base = pl.multiple_of(p * ROWS, ROWS)
        s = b_buf[c, j, pl.ds(base, half, stride=2), :]
        d = b_buf[c, j, pl.ds(base + 1, half, stride=2), :]
        pv = yz[c, j, pl.ds(p, 1), :]
        qv = yz[c, j, pl.ds(PLANES + p, 1), :]
        sv = yz[c, j, pl.ds(2 * PLANES + p, 1), :]
        dv = yz[c, j, pl.ds(3 * PLANES + p, 1), :]
        d = d + pa * (s + following(s, sv))
        dm = pv + pa * s[0:1]
        s = s + ub * (preceding(d, dm) + d)
        sn = sv + ub * (d[half - 1 :] + dv)
        sm = qv + ub * dm
        dm = dm + pg * (sm + s[0:1])
        d = d + pg * (s + following(s, sn))
        s = s + ue * (preceding(d, dm) + d)
        a_buf[c, j, pl.ds(base, half), :] = s
        a_buf[c, j, pl.ds(base + half, half), :] = d

    def y_planes(c, starts):
        for start in starts:
            def body(q, carry):
                for j in range(CHUNKS):
                    y_plane(c, start + q, j)
                return carry

            lax.fori_loop(0, 4, body, 0)

    parts = ((0, 4, 0, half), (4, 4, 0, half), (0, 8, half, half))

    def x_copy(side, c, part):
        j0, jn, r0, rn = parts[part]
        place = (c, slice(None), pl.ds(j0, jn), pl.ds(r0, rn), slice(None))
        return pltpu.make_async_remote_copy(
            src_ref=xs.at[(side, *place)],
            dst_ref=xr.at[(1 - side, *place)],
            send_sem=x_send.at[side, c, part],
            recv_sem=x_recv.at[1 - side, c, part],
            device_id={"wide": left if side == 0 else right},
            device_id_type=MESH,
        )

    def x_values(c):
        def body(j, carry):
            def plane(p):
                return a_buf[c, j, p * ROWS : p * ROWS + ROWS, :]

            p0 = plane(0)
            xs[0, c, 0, j] = p0
            xs[0, c, 1, j] = plane(1) + pa * (p0 + plane(2))
            e2 = plane(PLANES - 2)
            xs[1, c, 0, j] = plane(PLANES - 1) + pa * e2
            xs[1, c, 1, j] = e2 + ub * (plane(PLANES - 3) + pa * (plane(PLANES - 4) + e2))
            return carry

        lax.fori_loop(0, CHUNKS, body, 0)

    def x_ends(c):
        def body(j, carry):

            def plane(p):
                return a_buf[c, j, p * ROWS : p * ROWS + ROWS, :]

            @pl.when(jnp.logical_not(has_left))
            def _():
                xr[0, c, 0, j] = plane(1) + pa * plane(2)
                xr[0, c, 1, j] = plane(2) + ub * (plane(3) + pa * (plane(2) + plane(4)))

            @pl.when(jnp.logical_not(has_right))
            def _():
                xr[1, c, 0, j] = plane(PLANES - 2)
                xr[1, c, 1, j] = plane(PLANES - 3) + pa * (plane(PLANES - 4) + plane(PLANES - 2))

            return carry

        lax.fori_loop(0, CHUNKS, body, 0)

    def x_start(c, part):
        @pl.when(has_left)
        def _():
            x_copy(0, c, part).start()

        @pl.when(has_right)
        def _():
            x_copy(1, c, part).start()

    def x_arrived(c, part):
        @pl.when(has_left)
        def _():
            x_copy(1, c, part).wait_recv()

        @pl.when(has_right)
        def _():
            x_copy(0, c, part).wait_recv()

    def factor(band):
        shift = lax.shift_left(jnp.int32(1), 15 - e_ref[band - 1]).astype(F32)
        ups = 2 - 2 * (band // 4) - 2 * ((band // 2) % 2)
        return shift * (2.0**-15 * scaling**ups)

    def x_lift(c, by, bz):
        low_band, high_band = 2 * by + bz, 4 + 2 * by + bz
        high_scale = factor(high_band)
        low_scale = factor(low_band) if low_band else None

        def body(at, carry):
            k, t = at // 4, lax.rem(at, 4)
            j = 4 * bz + k
            row = pl.multiple_of(half * by + 8 * t, 8)

            def plane(p):
                return a_buf[c, j, pl.ds(pl.multiple_of(p * ROWS + row, 8), 8), :]

            s = [plane(2 * i) for i in range(8)]
            d = [plane(2 * i + 1) for i in range(8)]
            pv = xr[0, c, 0, j, pl.ds(row, 8), :]
            qv = xr[0, c, 1, j, pl.ds(row, 8), :]
            sv = xr[1, c, 0, j, pl.ds(row, 8), :]
            dv = xr[1, c, 1, j, pl.ds(row, 8), :]
            s.append(sv)
            d = [d[i] + pa * (s[i] + s[i + 1]) for i in range(8)]
            dm = pv + pa * s[0]
            sn = sv + ub * (d[7] + dv)
            sm = qv + ub * dm
            s = [s[i] + ub * ((d[i - 1] if i else dm) + d[i]) for i in range(8)]
            dm = dm + pg * (sm + s[0])
            s.append(sn)
            d = [d[i] + pg * (s[i] + s[i + 1]) for i in range(8)]
            s = [s[i] + ue * ((d[i - 1] if i else dm) + d[i]) for i in range(8)]
            lanes = pl.ds(pl.multiple_of(128 * k, 128), 128)
            rows = pl.ds(pl.multiple_of(8 * t, 8), 8)
            for i in range(8):
                v = d[i] * high_scale
                det_ref[c, high_band - 1, i, rows, lanes] = v - jnp.clip(v, -0.5, 0.5)
                if low_band:
                    v = s[i] * low_scale
                    det_ref[c, low_band - 1, i, rows, lanes] = v - jnp.clip(v, -0.5, 0.5)
                else:
                    lll[k, pl.ds(pl.multiple_of(half * i + 8 * t, 8), 8), :] = s[i] * (scaling * scaling)
            return carry

        lax.fori_loop(0, 16, body, 0)

    lane = lax.broadcasted_iota(jnp.int32, (8, 128), 1)
    low_half = lane < 64
    low_quarter = lax.rem(lane, 64) < 32

    xpos, zpos = wid // 4, lax.rem(wid, 4)

    def across(c, off, source):
        peer = lax.rem(xpos + off, 4)
        return pltpu.make_async_remote_copy(
            src_ref=lsend.at[pl.ds(4 * peer, 4), c],
            dst_ref=lmid.at[c, :, :, source],
            send_sem=l_send.at[0, c, off - 1],
            recv_sem=l_recv.at[0, c, source],
            device_id={"wide": 4 * peer + zpos},
            device_id_type=MESH,
        )

    def along(c, off, source):
        peer = lax.rem(zpos + off, 4)
        return pltpu.make_async_remote_copy(
            src_ref=lmid.at[c, peer],
            dst_ref=lrecv.at[c, :, :, source],
            send_sem=l_send.at[1, c, off - 1],
            recv_sem=l_recv.at[1, c, source],
            device_id={"wide": 4 * xpos + peer},
            device_id_type=MESH,
        )

    def l_pack(c):
        def body(k, carry):
            for g in range(8):
                v = [lll[k, pl.ds(4 * g + y, 8, stride=half), :] for y in range(4)]
                for a, b in ((0, 2), (1, 3)):
                    v[a], v[b] = (
                        jnp.where(low_half, v[a], pltpu.roll(v[b], 64, 1)),
                        jnp.where(low_half, pltpu.roll(v[a], 64, 1), v[b]),
                    )
                for a, b in ((0, 1), (2, 3)):
                    v[a], v[b] = (
                        jnp.where(low_quarter, v[a], pltpu.roll(v[b], 32, 1)),
                        jnp.where(low_quarter, pltpu.roll(v[a], 96, 1), v[b]),
                    )
                for y in range(4):
                    lsend[4 * k + y, c, g] = v[y]
            return carry

        lax.fori_loop(0, 4, body, 0)

        for off in (2, 1, 3):
            across(c, off, xpos).start()

        def own(z, carry):
            lmid[c, z, :, xpos] = lsend[4 * xpos + z, c]
            return carry

        lax.fori_loop(0, 4, own, 0)

    def l_turn(c):
        for off in (2, 1, 3):
            across(c, off, lax.rem(xpos + off, 4)).wait_recv()
        for off in (2, 1, 3):
            along(c, off, zpos).start()
        lrecv[c, :, :, zpos] = lmid[c, zpos]

    def l_take(c):
        for off in (2, 1, 3):
            along(c, off, lax.rem(zpos + off, 4)).wait_recv()

        def body(g, carry):
            block = lrecv[c, g].reshape((128, 128))
            ap_ref[c, pl.ds(pl.multiple_of(128 * g, 128), 128), :] = block.T
            return carry

        lax.fori_loop(0, 8, body, 0)

    y_values(0)
    load_w.wait()
    z_tiles(0, 0, 3)
    y_values(1)
    y_values(2)
    for c in range(COMPS):
        if c:
            z_tiles(c, 0, 3)
        z_halo(c)
        y_planes(c, (0, 12))
        x_values(c)
        x_start(c, 0)
        x_start(c, 1)
    x_start(0, 2)
    z_tiles(0, 1, 1)
    y_planes(0, (4, 8))
    x_ends(0)
    x_arrived(0, 0)
    x_lift(0, 0, 0)
    l_pack(0)
    z_tiles(1, 1, 1)
    y_planes(1, (4, 8))
    x_ends(1)
    x_arrived(1, 0)
    x_lift(1, 0, 0)
    l_pack(1)
    l_turn(0)
    x_start(1, 2)
    z_tiles(2, 1, 1)
    y_planes(2, (4, 8))
    x_ends(2)
    x_arrived(2, 0)
    x_lift(2, 0, 0)
    l_pack(2)
    l_turn(1)
    x_start(2, 2)
    x_arrived(0, 1)
    x_lift(0, 0, 1)
    l_turn(2)
    x_arrived(1, 1)
    x_lift(1, 0, 1)
    x_arrived(2, 1)
    x_lift(2, 0, 1)
    for c in range(COMPS):
        x_arrived(c, 2)
        x_lift(c, 1, 0)
        x_lift(c, 1, 1)
        l_take(c)

    for c in range(COMPS):
        @pl.when(has_up)
        def _():
            y_copy(0, c).wait_send()

        @pl.when(has_down)
        def _():
            y_copy(1, c).wait_send()

        for part in range(3):
            @pl.when(has_left)
            def _():
                x_copy(0, c, part).wait_send()

            @pl.when(has_right)
            def _():
                x_copy(1, c, part).wait_send()

        for off in (1, 2, 3):
            across(c, off, xpos).wait_send()
            along(c, off, zpos).wait_send()


def local(n_narrow, n_wide, velocity, exponents):
    cells = velocity.reshape((COMPS, PLANES * ROWS, DEPTH))
    approx, details = pl.pallas_call(
        functools.partial(kernel, n_narrow, n_wide),
        out_shape=(
            pltpu.VMEM((COMPS, 1024, 128), F32),
            pltpu.VMEM((COMPS, 7, PLANES // 2, ROWS // 2, DEPTH // 2), F32),
        ),
        in_specs=[
            pl.BlockSpec(memory_space=pl.ANY),
            pl.BlockSpec(memory_space=pltpu.SMEM),
            pl.BlockSpec(memory_space=pl.ANY),
        ],
        out_specs=(
            pl.BlockSpec(memory_space=pltpu.VMEM),
            pl.BlockSpec(memory_space=pltpu.VMEM),
        ),
        scratch_shapes=[
            pltpu.VMEM((COMPS, CHUNKS, PLANES * ROWS, 128), F32),
            pltpu.VMEM((COMPS, CHUNKS, PLANES * ROWS, 128), F32),
            pltpu.VMEM((2 * TILE, DEPTH), BF16),
            pltpu.VMEM((3, 2, 512, 256), BF16),
            pltpu.VMEM((2, COMPS, CHUNKS, 2 * PLANES, 128), F32),
            pltpu.VMEM((2, COMPS, CHUNKS, 2 * PLANES, 128), F32),
            pltpu.VMEM((COMPS, CHUNKS, 4 * PLANES, 128), F32),
            pltpu.VMEM((2, COMPS, 2, CHUNKS, ROWS, 128), F32),
            pltpu.VMEM((2, COMPS, 2, CHUNKS, ROWS, 128), F32),
            pltpu.VMEM((4, 256, 128), F32),
            pltpu.VMEM((16, COMPS, 8, 8, 128), F32),
            pltpu.VMEM((COMPS, 4, 8, 4, 8, 128), F32),
            pltpu.VMEM((COMPS, 8, 4, 4, 8, 128), F32),
            pltpu.SemaphoreType.DMA((COMPS, CHUNKS)),
            pltpu.SemaphoreType.DMA,
            pltpu.SemaphoreType.DMA((2, COMPS)),
            pltpu.SemaphoreType.DMA((2, COMPS)),
            pltpu.SemaphoreType.DMA((2, COMPS, 3)),
            pltpu.SemaphoreType.DMA((2, COMPS, 3)),
            pltpu.SemaphoreType.DMA((2, COMPS, 3)),
            pltpu.SemaphoreType.DMA((2, COMPS, 4)),
        ],
        compiler_params=pltpu.CompilerParams(
            collective_id=0, has_side_effects=True, vmem_limit_bytes=48 * 1024 * 1024
        ),
        cost_estimate=pl.CostEstimate(
            flops=10_000_000_000, bytes_accessed=26_000_000, transcendentals=0
        ),
    )(cells, exponents, jnp.asarray(z_weights()))
    approx = approx.reshape((COMPS, ROWS // 2, 32, 128))
    return jnp.transpose(approx, (0, 3, 1, 2)), details


def solution(mesh):
    placed = (P(None, "wide", "narrow", None), P())
    return jax.shard_map(
        functools.partial(local, mesh.shape["narrow"], mesh.shape["wide"]),
        mesh=mesh,
        in_specs=placed,
        out_specs=(P(None, None, "narrow", "wide"), P(None, None, "wide", "narrow", None)),
        check_vma=False,
    )
```

```python
import functools

import jax
import jax.numpy as jnp
import ml_dtypes
import numpy as np
from jax import lax
from jax.experimental import pallas as pl
from jax.experimental.pallas import tpu as pltpu
from jax.sharding import PartitionSpec as P

MESH = pl.DeviceIdType.MESH
F32 = jnp.float32
BF16 = jnp.bfloat16

pa = -1.586134342
ub = -0.05298011854
pg = 0.8829110762
ue = 0.4435068522
scaling = 1.149604398

COMPS = 3
PLANES = 16
ROWS = 64
DEPTH = 1024
CHUNKS = DEPTH // 128
TILE = 256
WINDOW_START = (0, 128, 384, 512)
WINDOW_KIND = (0, 1, 1, 2)


def z_weights():
    ext = np.pad(np.eye(DEPTH), ((0, 0), (4, 4)), mode="reflect")
    s, d = ext[:, 0::2], ext[:, 1::2]
    d = d[:, :-1] + pa * (s[:, :-1] + s[:, 1:])
    s = s[:, 1:-1] + ub * (d[:, :-1] + d[:, 1:])
    d = d[:, 1:-1] + pg * (s[:, :-1] + s[:, 1:])
    s = s[:, 1:-1] + ue * (d[:, :-1] + d[:, 1:])
    low, high = s * scaling, d[:, 1:] / scaling
    kinds = []
    for k in (0, 1, 3):
        rows = slice(WINDOW_START[k], WINDOW_START[k] + 512)
        cols = slice(128 * k, 128 * k + 128)
        kinds.append(np.concatenate([low[rows, cols], high[rows, cols]], 1))
    full = np.stack(kinds)
    head = full.astype(np.float32).astype(ml_dtypes.bfloat16)
    rest = (full - head.astype(np.float64)).astype(np.float32).astype(ml_dtypes.bfloat16)
    return np.stack([head, rest], 1)


def kernel(
    n_narrow, n_wide,
    x_ref, e_ref, w_ref, ap_ref, det_ref,
    a_buf, b_buf, hl, wv, ys, yr, yz, xs, xr, ms, mr, lll, lsend, lmid, lrecv,
    load_sem, w_sem, y_send, y_recv, x_send, x_recv, m_send, m_recv, l_send, l_recv,
):
    nar = lax.axis_index("narrow")
    wid = lax.axis_index("wide")
    up = lax.rem(nar + n_narrow - 1, n_narrow)
    down = lax.rem(nar + 1, n_narrow)
    left = lax.rem(wid + n_wide - 1, n_wide)
    right = lax.rem(wid + 1, n_wide)
    has_up, has_down = nar > 0, nar < n_narrow - 1
    has_left, has_right = wid > 0, wid < n_wide - 1

    def load(c, j):
        return pltpu.make_async_copy(
            x_ref.at[c, :, pl.ds(128 * j, 128)], a_buf.at[c, j], load_sem.at[c, j]
        )

    load_w = pltpu.make_async_copy(w_ref, wv, w_sem)
    for j in range(CHUNKS):
        load(0, j).start()
    load_w.start()

    barrier = pltpu.get_barrier_semaphore()

    def greet(off, carry):
        pl.semaphore_signal(
            barrier, inc=1, device_id={"wide": lax.rem(wid + off, n_wide)}, device_id_type=MESH
        )
        return carry

    lax.fori_loop(1, n_wide, greet, 0)

    @pl.when(has_up)
    def _():
        pl.semaphore_signal(barrier, inc=1, device_id={"narrow": up}, device_id_type=MESH)

    @pl.when(has_down)
    def _():
        pl.semaphore_signal(barrier, inc=1, device_id={"narrow": down}, device_id_type=MESH)

    pl.semaphore_wait(
        barrier, n_wide - 1 + has_up.astype(jnp.int32) + has_down.astype(jnp.int32)
    )

    def y_copy(side, c):
        return pltpu.make_async_remote_copy(
            src_ref=ys.at[side, c],
            dst_ref=yr.at[1 - side, c],
            send_sem=y_send.at[side, c],
            recv_sem=y_recv.at[1 - side, c],
            device_id={"narrow": up if side == 0 else down},
            device_id_type=MESH,
        )

    def loaded(c):
        for j in range(CHUNKS):
            load(c, j).wait()
        if c + 1 < COMPS:
            for j in range(CHUNKS):
                load(c + 1, j).start()

    def y_values(c):
        def body(j, carry):
            def row(r):
                return a_buf[c, j, pl.ds(r, PLANES, stride=ROWS), :]

            r0, r1, r2 = row(0), row(1), row(2)
            e0, e1, e2, e3 = row(ROWS - 4), row(ROWS - 3), row(ROWS - 2), row(ROWS - 1)
            before_last = e1 + pa * (e0 + e2)
            ys[0, c, j, 0:PLANES, :] = r0
            ys[0, c, j, PLANES:, :] = r1 + pa * (r0 + r2)
            ys[1, c, j, 0:PLANES, :] = e3 + pa * e2
            ys[1, c, j, PLANES:, :] = e2 + ub * before_last

            @pl.when(jnp.logical_not(has_up))
            def _():
                r3, r4 = row(3), row(4)
                yr[0, c, j, 0:PLANES, :] = r1 + pa * r2
                yr[0, c, j, PLANES:, :] = r2 + ub * (r3 + pa * (r2 + r4))

            @pl.when(jnp.logical_not(has_down))
            def _():
                yr[1, c, j, 0:PLANES, :] = e2
                yr[1, c, j, PLANES:, :] = before_last

            return carry

        lax.fori_loop(0, CHUNKS, body, 0)

        @pl.when(has_up)
        def _():
            y_copy(0, c).start()

        @pl.when(has_down)
        def _():
            y_copy(1, c).start()

    def z_rows(m, get, put):
        for j in range(CHUNKS):
            value = get(j)
            head = value.astype(BF16)
            hl[0:m, 128 * j : 128 * j + 128] = head
            hl[m : 2 * m, 128 * j : 128 * j + 128] = (value - head.astype(F32)).astype(BF16)
        for k in range(CHUNKS // 2):
            start, kind = WINDOW_START[k], WINDOW_KIND[k]
            both = jnp.dot(
                hl[0 : 2 * m, start : start + 512], wv[kind, 0], preferred_element_type=F32
            )
            rest = jnp.dot(hl[0:m, start : start + 512], wv[kind, 1], preferred_element_type=F32)
            out = both[:m] + (both[m:] + rest)
            put(k, out[:, :128])
            put(CHUNKS // 2 + k, out[:, 128:])

    def z_tiles(c, first, step, count=2):
        def body(t, carry):
            base = pl.multiple_of((first + step * t) * TILE, TILE)

            def put(j, value):
                b_buf[c, j, pl.ds(base, TILE), :] = value

            z_rows(TILE, lambda j: a_buf[c, j, pl.ds(base, TILE), :], put)
            return carry

        lax.fori_loop(0, count, body, 0)

    def y_arrived(c):
        @pl.when(has_up)
        def _():
            y_copy(1, c).wait_recv()

        @pl.when(has_down)
        def _():
            y_copy(0, c).wait_recv()

    def z_halo(c):
        def put(j, value):
            yz[c, j] = value

        z_rows(
            4 * PLANES,
            lambda j: jnp.concatenate([yr[0, c, j], yr[1, c, j]], 0),
            put,
        )

    half = ROWS // 2
    row_at = lax.broadcasted_iota(jnp.int32, (half, 128), 0)

    def following(value, last):
        return jnp.where(row_at == half - 1, last, pltpu.roll(value, half - 1, 0))

    def preceding(value, first):
        return jnp.where(row_at == 0, first, pltpu.roll(value, 1, 0))

    def y_plane(c, p, j):
        base = pl.multiple_of(p * ROWS, ROWS)
        s, d = y_rows(c, j, base, [yz[c, j, pl.ds(PLANES * kind + p, 1), :] for kind in range(4)])
        a_buf[c, j, pl.ds(base, half), :] = s
        a_buf[c, j, pl.ds(base + half, half), :] = d

    def y_rows(c, j, base, rim):
        s = b_buf[c, j, pl.ds(base, half, stride=2), :]
        d = b_buf[c, j, pl.ds(base + 1, half, stride=2), :]
        pv, qv, sv, dv = rim
        d = d + pa * (s + following(s, sv))
        dm = pv + pa * s[0:1]
        s = s + ub * (preceding(d, dm) + d)
        sn = sv + ub * (d[half - 1 :] + dv)
        sm = qv + ub * dm
        dm = dm + pg * (sm + s[0:1])
        d = d + pg * (s + following(s, sn))
        s = s + ue * (preceding(d, dm) + d)
        return s, d

    def y_planes(c, starts):
        for start in starts:
            def body(q, carry):
                for j in range(CHUNKS):
                    y_plane(c, start + q, j)
                return carry

            lax.fori_loop(0, 4, body, 0)

    parts = ((0, 4, 0, half), (4, 4, 0, half), (0, 8, half, half), (0, 8, 0, ROWS))

    def x_copy(side, c, part):
        j0, jn, r0, rn = parts[part]
        place = (c, slice(None), pl.ds(j0, jn), pl.ds(r0, rn), slice(None))
        return pltpu.make_async_remote_copy(
            src_ref=xs.at[(side, *place)],
            dst_ref=xr.at[(1 - side, *place)],
            send_sem=x_send.at[side, c, part],
            recv_sem=x_recv.at[1 - side, c, part],
            device_id={"wide": left if side == 0 else right},
            device_id_type=MESH,
        )

    def x_values(c):
        def body(j, carry):
            def plane(p):
                return a_buf[c, j, p * ROWS : p * ROWS + ROWS, :]

            p0 = plane(0)
            xs[0, c, 0, j] = p0
            xs[0, c, 1, j] = plane(1) + pa * (p0 + plane(2))
            e2 = plane(PLANES - 2)
            xs[1, c, 0, j] = plane(PLANES - 1) + pa * e2
            xs[1, c, 1, j] = e2 + ub * (plane(PLANES - 3) + pa * (plane(PLANES - 4) + e2))
            return carry

        lax.fori_loop(0, CHUNKS, body, 0)

    def x_ends(c):
        def body(j, carry):

            def plane(p):
                return a_buf[c, j, p * ROWS : p * ROWS + ROWS, :]

            @pl.when(jnp.logical_not(has_left))
            def _():
                xr[0, c, 0, j] = plane(1) + pa * plane(2)
                xr[0, c, 1, j] = plane(2) + ub * (plane(3) + pa * (plane(2) + plane(4)))

            @pl.when(jnp.logical_not(has_right))
            def _():
                xr[1, c, 0, j] = plane(PLANES - 2)
                xr[1, c, 1, j] = plane(PLANES - 3) + pa * (plane(PLANES - 4) + plane(PLANES - 2))

            return carry

        lax.fori_loop(0, CHUNKS, body, 0)

    def x_start(c, part):
        @pl.when(has_left)
        def _():
            x_copy(0, c, part).start()

        @pl.when(has_right)
        def _():
            x_copy(1, c, part).start()

    def x_arrived(c, part):
        @pl.when(has_left)
        def _():
            x_copy(1, c, part).wait_recv()

        @pl.when(has_right)
        def _():
            x_copy(0, c, part).wait_recv()

    def m_copy(side):
        return pltpu.make_async_remote_copy(
            src_ref=ms.at[side],
            dst_ref=mr.at[1 - side],
            send_sem=m_send.at[side],
            recv_sem=m_recv.at[1 - side],
            device_id={"wide": left if side == 0 else right},
            device_id_type=MESH,
        )

    def m_values():
        def body(j, carry):
            for kind in range(4):
                def row(p):
                    return yr[kind // 2, 0, j, pl.ds(PLANES * (kind % 2) + p, 1), :]

                e2 = row(PLANES - 2)
                ms[0, j, kind : kind + 1, :] = row(0)
                ms[0, j, 4 + kind : 5 + kind, :] = row(1) + pa * (row(0) + row(2))
                ms[1, j, kind : kind + 1, :] = row(PLANES - 1) + pa * e2
                ms[1, j, 4 + kind : 5 + kind, :] = e2 + ub * (
                    row(PLANES - 3) + pa * (row(PLANES - 4) + e2)
                )
            return carry

        lax.fori_loop(0, CHUNKS, body, 0)

        @pl.when(has_left)
        def _():
            m_copy(0).start()

        @pl.when(has_right)
        def _():
            m_copy(1).start()

    def m_lift():
        x_arrived(0, 3)

        @pl.when(has_left)
        def _():
            m_copy(1).wait_recv()

        @pl.when(has_right)
        def _():
            m_copy(0).wait_recv()

        def get(j):
            return jnp.concatenate(
                [xr[0, 0, 0, j], xr[0, 0, 1, j], xr[1, 0, 0, j], xr[1, 0, 1, j], mr[0, j], mr[1, j]], 0
            )

        def put(j, value):
            b_buf[0, j, 0 : TILE + 16, :] = value

        z_rows(TILE + 16, get, put)

        def side_lift(side):
            def body(j, carry):
                for combo in range(2):
                    at = TILE + 8 * side + 4 * combo
                    s, d = y_rows(
                        0, j, ROWS * (2 * side + combo),
                        [b_buf[0, j, at + kind : at + kind + 1, :] for kind in range(4)],
                    )
                    xr[side, 0, combo, j, 0:half, :] = s
                    xr[side, 0, combo, j, half:, :] = d
                return carry

            lax.fori_loop(0, CHUNKS, body, 0)

        @pl.when(has_left)
        def _():
            side_lift(0)

        @pl.when(has_right)
        def _():
            side_lift(1)

    def factor(band):
        shift = lax.shift_left(jnp.int32(1), 15 - e_ref[band - 1]).astype(F32)
        ups = 2 - 2 * (band // 4) - 2 * ((band // 2) % 2)
        return shift * (2.0**-15 * scaling**ups)

    def x_lift(c, by, bz):
        low_band, high_band = 2 * by + bz, 4 + 2 * by + bz
        high_scale = factor(high_band)
        low_scale = factor(low_band) if low_band else None

        def body(at, carry):
            k, t = at // 4, lax.rem(at, 4)
            j = 4 * bz + k
            row = pl.multiple_of(half * by + 8 * t, 8)

            def plane(p):
                return a_buf[c, j, pl.ds(pl.multiple_of(p * ROWS + row, 8), 8), :]

            s = [plane(2 * i) for i in range(8)]
            d = [plane(2 * i + 1) for i in range(8)]
            pv = xr[0, c, 0, j, pl.ds(row, 8), :]
            qv = xr[0, c, 1, j, pl.ds(row, 8), :]
            sv = xr[1, c, 0, j, pl.ds(row, 8), :]
            dv = xr[1, c, 1, j, pl.ds(row, 8), :]
            s.append(sv)
            d = [d[i] + pa * (s[i] + s[i + 1]) for i in range(8)]
            dm = pv + pa * s[0]
            sn = sv + ub * (d[7] + dv)
            sm = qv + ub * dm
            s = [s[i] + ub * ((d[i - 1] if i else dm) + d[i]) for i in range(8)]
            dm = dm + pg * (sm + s[0])
            s.append(sn)
            d = [d[i] + pg * (s[i] + s[i + 1]) for i in range(8)]
            s = [s[i] + ue * ((d[i - 1] if i else dm) + d[i]) for i in range(8)]
            lanes = pl.ds(pl.multiple_of(128 * k, 128), 128)
            rows = pl.ds(pl.multiple_of(8 * t, 8), 8)
            for i in range(8):
                v = d[i] * high_scale
                det_ref[c, high_band - 1, i, rows, lanes] = v - jnp.clip(v, -0.5, 0.5)
                if low_band:
                    v = s[i] * low_scale
                    det_ref[c, low_band - 1, i, rows, lanes] = v - jnp.clip(v, -0.5, 0.5)
                else:
                    lll[k, pl.ds(pl.multiple_of(half * i + 8 * t, 8), 8), :] = s[i] * (scaling * scaling)
            return carry

        lax.fori_loop(0, 16, body, 0)

    lane = lax.broadcasted_iota(jnp.int32, (8, 128), 1)
    low_half = lane < 64
    low_quarter = lax.rem(lane, 64) < 32

    xpos, zpos = wid // 4, lax.rem(wid, 4)

    def across(c, off, source):
        peer = lax.rem(xpos + off, 4)
        return pltpu.make_async_remote_copy(
            src_ref=lsend.at[pl.ds(4 * peer, 4), c],
            dst_ref=lmid.at[c, :, :, source],
            send_sem=l_send.at[0, c, off - 1],
            recv_sem=l_recv.at[0, c, source],
            device_id={"wide": 4 * peer + zpos},
            device_id_type=MESH,
        )

    def along(c, off, source):
        peer = lax.rem(zpos + off, 4)
        return pltpu.make_async_remote_copy(
            src_ref=lmid.at[c, peer],
            dst_ref=lrecv.at[c, :, :, source],
            send_sem=l_send.at[1, c, off - 1],
            recv_sem=l_recv.at[1, c, source],
            device_id={"wide": 4 * xpos + peer},
            device_id_type=MESH,
        )

    def l_pack(c):
        def body(k, carry):
            for g in range(8):
                v = [lll[k, pl.ds(4 * g + y, 8, stride=half), :] for y in range(4)]
                for a, b in ((0, 2), (1, 3)):
                    v[a], v[b] = (
                        jnp.where(low_half, v[a], pltpu.roll(v[b], 64, 1)),
                        jnp.where(low_half, pltpu.roll(v[a], 64, 1), v[b]),
                    )
                for a, b in ((0, 1), (2, 3)):
                    v[a], v[b] = (
                        jnp.where(low_quarter, v[a], pltpu.roll(v[b], 32, 1)),
                        jnp.where(low_quarter, pltpu.roll(v[a], 96, 1), v[b]),
                    )
                for y in range(4):
                    lsend[4 * k + y, c, g] = v[y]
            return carry

        lax.fori_loop(0, 4, body, 0)

        for off in (2, 1, 3):
            across(c, off, xpos).start()

        def own(z, carry):
            lmid[c, z, :, xpos] = lsend[4 * xpos + z, c]
            return carry

        lax.fori_loop(0, 4, own, 0)

    def l_turn(c):
        for off in (2, 1, 3):
            across(c, off, lax.rem(xpos + off, 4)).wait_recv()
        for off in (2, 1, 3):
            along(c, off, zpos).start()
        lrecv[c, :, :, zpos] = lmid[c, zpos]

    def l_take(c):
        for off in (2, 1, 3):
            along(c, off, lax.rem(zpos + off, 4)).wait_recv()

        def body(g, carry):
            block = lrecv[c, g].reshape((128, 128))
            ap_ref[c, pl.ds(pl.multiple_of(128 * g, 128), 128), :] = block.T
            return carry

        lax.fori_loop(0, 8, body, 0)

    loaded(0)
    x_values(0)
    x_start(0, 3)
    loaded(1)
    y_values(1)
    y_values(0)
    load_w.wait()
    z_tiles(1, 0, 3)
    loaded(2)
    y_values(2)
    y_arrived(1)
    z_halo(1)
    y_planes(1, (0, 12))
    x_values(1)
    x_start(1, 0)
    x_start(1, 1)
    y_arrived(0)
    m_values()
    z_tiles(2, 0, 3)
    y_arrived(2)
    z_halo(2)
    y_planes(2, (0, 12))
    x_values(2)
    x_start(2, 0)
    x_start(2, 1)
    z_tiles(0, 0, 1, 4)
    z_halo(0)
    y_planes(0, (0, 4, 8, 12))
    m_lift()
    x_ends(0)
    x_lift(0, 0, 0)
    l_pack(0)
    x_start(1, 2)
    x_lift(0, 0, 1)
    z_tiles(1, 1, 1)
    y_planes(1, (4, 8))
    l_turn(0)
    x_ends(1)
    x_arrived(1, 0)
    x_lift(1, 0, 0)
    l_pack(1)
    z_tiles(2, 1, 1)
    y_planes(2, (4, 8))
    l_turn(1)
    x_start(2, 2)
    x_ends(2)
    x_arrived(2, 0)
    x_lift(2, 0, 0)
    l_pack(2)
    x_lift(0, 1, 0)
    l_turn(2)
    x_lift(0, 1, 1)
    for c in (1, 2):
        x_arrived(c, 1)
        x_lift(c, 0, 1)
    x_arrived(1, 2)
    x_lift(1, 1, 0)
    x_lift(1, 1, 1)
    l_take(0)
    l_take(1)
    x_arrived(2, 2)
    x_lift(2, 1, 0)
    x_lift(2, 1, 1)
    l_take(2)

    for c in range(COMPS):
        @pl.when(has_up)
        def _():
            y_copy(0, c).wait_send()

        @pl.when(has_down)
        def _():
            y_copy(1, c).wait_send()

        for part in (range(3) if c else (3,)):
            @pl.when(has_left)
            def _():
                x_copy(0, c, part).wait_send()

            @pl.when(has_right)
            def _():
                x_copy(1, c, part).wait_send()

        if c == 0:
            @pl.when(has_left)
            def _():
                m_copy(0).wait_send()

            @pl.when(has_right)
            def _():
                m_copy(1).wait_send()

        for off in (1, 2, 3):
            across(c, off, xpos).wait_send()
            along(c, off, zpos).wait_send()


def local(n_narrow, n_wide, velocity, exponents):
    cells = velocity.reshape((COMPS, PLANES * ROWS, DEPTH))
    approx, details = pl.pallas_call(
        functools.partial(kernel, n_narrow, n_wide),
        out_shape=(
            pltpu.VMEM((COMPS, 1024, 128), F32),
            pltpu.VMEM((COMPS, 7, PLANES // 2, ROWS // 2, DEPTH // 2), F32),
        ),
        in_specs=[
            pl.BlockSpec(memory_space=pl.ANY),
            pl.BlockSpec(memory_space=pltpu.SMEM),
            pl.BlockSpec(memory_space=pl.ANY),
        ],
        out_specs=(
            pl.BlockSpec(memory_space=pltpu.VMEM),
            pl.BlockSpec(memory_space=pltpu.VMEM),
        ),
        scratch_shapes=[
            pltpu.VMEM((COMPS, CHUNKS, PLANES * ROWS, 128), F32),
            pltpu.VMEM((COMPS, CHUNKS, PLANES * ROWS, 128), F32),
            pltpu.VMEM((2 * TILE + 32, DEPTH), BF16),
            pltpu.VMEM((3, 2, 512, 256), BF16),
            pltpu.VMEM((2, COMPS, CHUNKS, 2 * PLANES, 128), F32),
            pltpu.VMEM((2, COMPS, CHUNKS, 2 * PLANES, 128), F32),
            pltpu.VMEM((COMPS, CHUNKS, 4 * PLANES, 128), F32),
            pltpu.VMEM((2, COMPS, 2, CHUNKS, ROWS, 128), F32),
            pltpu.VMEM((2, COMPS, 2, CHUNKS, ROWS, 128), F32),
            pltpu.VMEM((2, CHUNKS, 8, 128), F32),
            pltpu.VMEM((2, CHUNKS, 8, 128), F32),
            pltpu.VMEM((4, 256, 128), F32),
            pltpu.VMEM((16, COMPS, 8, 8, 128), F32),
            pltpu.VMEM((COMPS, 4, 8, 4, 8, 128), F32),
            pltpu.VMEM((COMPS, 8, 4, 4, 8, 128), F32),
            pltpu.SemaphoreType.DMA((COMPS, CHUNKS)),
            pltpu.SemaphoreType.DMA,
            pltpu.SemaphoreType.DMA((2, COMPS)),
            pltpu.SemaphoreType.DMA((2, COMPS)),
            pltpu.SemaphoreType.DMA((2, COMPS, 4)),
            pltpu.SemaphoreType.DMA((2, COMPS, 4)),
            pltpu.SemaphoreType.DMA((2,)),
            pltpu.SemaphoreType.DMA((2,)),
            pltpu.SemaphoreType.DMA((2, COMPS, 3)),
            pltpu.SemaphoreType.DMA((2, COMPS, 4)),
        ],
        compiler_params=pltpu.CompilerParams(
            collective_id=0, has_side_effects=True, vmem_limit_bytes=48 * 1024 * 1024
        ),
        cost_estimate=pl.CostEstimate(
            flops=10_000_000_000, bytes_accessed=26_000_000, transcendentals=0
        ),
    )(cells, exponents, jnp.asarray(z_weights()))
    approx = approx.reshape((COMPS, ROWS // 2, 32, 128))
    return jnp.transpose(approx, (0, 3, 1, 2)), details


def solution(mesh):
    placed = (P(None, "wide", "narrow", None), P())
    return jax.shard_map(
        functools.partial(local, mesh.shape["narrow"], mesh.shape["wide"]),
        mesh=mesh,
        in_specs=placed,
        out_specs=(P(None, None, "narrow", "wide"), P(None, None, "wide", "narrow", None)),
        check_vma=False,
    )
```

```python
import functools

import jax
import jax.numpy as jnp
import ml_dtypes
import numpy as np
from jax import lax
from jax.experimental import pallas as pl
from jax.experimental.pallas import tpu as pltpu
from jax.sharding import PartitionSpec as P

MESH = pl.DeviceIdType.MESH
F32 = jnp.float32
BF16 = jnp.bfloat16

pa = -1.586134342
ub = -0.05298011854
pg = 0.8829110762
ue = 0.4435068522
scaling = 1.149604398

COMPS = 3
PLANES = 16
ROWS = 64
DEPTH = 1024
CHUNKS = DEPTH // 128
TILE = 256
WINDOW_START = (0, 128, 384, 512)
WINDOW_KIND = (0, 1, 1, 2)


def z_weights():
    ext = np.pad(np.eye(DEPTH), ((0, 0), (4, 4)), mode="reflect")
    s, d = ext[:, 0::2], ext[:, 1::2]
    d = d[:, :-1] + pa * (s[:, :-1] + s[:, 1:])
    s = s[:, 1:-1] + ub * (d[:, :-1] + d[:, 1:])
    d = d[:, 1:-1] + pg * (s[:, :-1] + s[:, 1:])
    s = s[:, 1:-1] + ue * (d[:, :-1] + d[:, 1:])
    low, high = s * scaling, d[:, 1:] / scaling
    kinds = []
    for k in (0, 1, 3):
        rows = slice(WINDOW_START[k], WINDOW_START[k] + 512)
        cols = slice(128 * k, 128 * k + 128)
        kinds.append(np.concatenate([low[rows, cols], high[rows, cols]], 1))
    full = np.stack(kinds)
    head = full.astype(np.float32).astype(ml_dtypes.bfloat16)
    rest = (full - head.astype(np.float64)).astype(np.float32).astype(ml_dtypes.bfloat16)
    return np.stack([head, rest], 1)


def factor(e_ref, band):
    shift = lax.shift_left(jnp.int32(1), 15 - e_ref[band - 1]).astype(F32)
    ups = 2 - 2 * (band // 4) - 2 * ((band // 2) % 2)
    return shift * (2.0**-15 * scaling**ups)


def x_lift_quarter(cells, rims, e_ref, c, by, bz, put, low_put):
    half = ROWS // 2
    low_band, high_band = 2 * by + bz, 4 + 2 * by + bz
    high_scale = factor(e_ref, high_band)
    low_scale = factor(e_ref, low_band) if low_band else None

    def body(at, carry):
        k, t = at // 4, lax.rem(at, 4)
        j = 4 * bz + k
        row = pl.multiple_of(half * by + 8 * t, 8)

        def plane(p):
            return cells[j, pl.ds(pl.multiple_of(p * ROWS + row, 8), 8), :]

        s = [plane(2 * i) for i in range(8)]
        d = [plane(2 * i + 1) for i in range(8)]
        pv = rims[0, c, 0, j, pl.ds(row, 8), :]
        qv = rims[0, c, 1, j, pl.ds(row, 8), :]
        sv = rims[1, c, 0, j, pl.ds(row, 8), :]
        dv = rims[1, c, 1, j, pl.ds(row, 8), :]
        s.append(sv)
        d = [d[i] + pa * (s[i] + s[i + 1]) for i in range(8)]
        dm = pv + pa * s[0]
        sn = sv + ub * (d[7] + dv)
        sm = qv + ub * dm
        s = [s[i] + ub * ((d[i - 1] if i else dm) + d[i]) for i in range(8)]
        dm = dm + pg * (sm + s[0])
        s.append(sn)
        d = [d[i] + pg * (s[i] + s[i + 1]) for i in range(8)]
        s = [s[i] + ue * ((d[i - 1] if i else dm) + d[i]) for i in range(8)]
        lanes = pl.ds(pl.multiple_of(128 * k, 128), 128)
        rows = pl.ds(pl.multiple_of(8 * t, 8), 8)
        for i in range(8):
            v = d[i] * high_scale
            put(high_band, i, rows, lanes, v - jnp.clip(v, -0.5, 0.5))
            if low_band:
                v = s[i] * low_scale
                put(low_band, i, rows, lanes, v - jnp.clip(v, -0.5, 0.5))
            else:
                low_put(k, t, i, s[i] * (scaling * scaling))
        return carry

    lax.fori_loop(0, 16, body, 0)


def turn_blocks(received, c, put):
    def body(g, carry):
        put(pl.ds(pl.multiple_of(128 * g, 128), 128), received[c, g].reshape((128, 128)).T)
        return carry

    lax.fori_loop(0, 8, body, 0)


def kernel(
    n_narrow, n_wide,
    x_ref, e_ref, w_ref, ap_ref, det_ref, a_last, xr, lrecv,
    a_first, a_second, b_buf, hl, wv, ys, yr, yz, xs, ms, mr, lll, lsend, lmid,
    load_sem, w_sem, y_send, y_recv, x_send, x_recv, m_send, m_recv, l_send, l_recv,
):
    cells = (a_first, a_second, a_last)
    nar = lax.axis_index("narrow")
    wid = lax.axis_index("wide")
    up = lax.rem(nar + n_narrow - 1, n_narrow)
    down = lax.rem(nar + 1, n_narrow)
    left = lax.rem(wid + n_wide - 1, n_wide)
    right = lax.rem(wid + 1, n_wide)
    has_up, has_down = nar > 0, nar < n_narrow - 1
    has_left, has_right = wid > 0, wid < n_wide - 1

    def load(c, j):
        return pltpu.make_async_copy(
            x_ref.at[c, :, pl.ds(128 * j, 128)], cells[c].at[j], load_sem.at[c, j]
        )

    load_w = pltpu.make_async_copy(w_ref, wv, w_sem)
    for j in range(CHUNKS):
        load(0, j).start()
    load_w.start()

    barrier = pltpu.get_barrier_semaphore()

    def greet(off, carry):
        pl.semaphore_signal(
            barrier, inc=1, device_id={"wide": lax.rem(wid + off, n_wide)}, device_id_type=MESH
        )
        return carry

    lax.fori_loop(1, n_wide, greet, 0)

    @pl.when(has_up)
    def _():
        pl.semaphore_signal(barrier, inc=1, device_id={"narrow": up}, device_id_type=MESH)

    @pl.when(has_down)
    def _():
        pl.semaphore_signal(barrier, inc=1, device_id={"narrow": down}, device_id_type=MESH)

    pl.semaphore_wait(
        barrier, n_wide - 1 + has_up.astype(jnp.int32) + has_down.astype(jnp.int32)
    )

    def y_copy(side, c):
        return pltpu.make_async_remote_copy(
            src_ref=ys.at[side, c],
            dst_ref=yr.at[1 - side, c],
            send_sem=y_send.at[side, c],
            recv_sem=y_recv.at[1 - side, c],
            device_id={"narrow": up if side == 0 else down},
            device_id_type=MESH,
        )

    def loaded(c):
        for j in range(CHUNKS):
            load(c, j).wait()
        if c + 1 < COMPS:
            for j in range(CHUNKS):
                load(c + 1, j).start()

    def y_values(c):
        def body(j, carry):
            def row(r):
                return cells[c][j, pl.ds(r, PLANES, stride=ROWS), :]

            r0, r1, r2 = row(0), row(1), row(2)
            e0, e1, e2, e3 = row(ROWS - 4), row(ROWS - 3), row(ROWS - 2), row(ROWS - 1)
            before_last = e1 + pa * (e0 + e2)
            ys[0, c, j, 0:PLANES, :] = r0
            ys[0, c, j, PLANES:, :] = r1 + pa * (r0 + r2)
            ys[1, c, j, 0:PLANES, :] = e3 + pa * e2
            ys[1, c, j, PLANES:, :] = e2 + ub * before_last

            @pl.when(jnp.logical_not(has_up))
            def _():
                r3, r4 = row(3), row(4)
                yr[0, c, j, 0:PLANES, :] = r1 + pa * r2
                yr[0, c, j, PLANES:, :] = r2 + ub * (r3 + pa * (r2 + r4))

            @pl.when(jnp.logical_not(has_down))
            def _():
                yr[1, c, j, 0:PLANES, :] = e2
                yr[1, c, j, PLANES:, :] = before_last

            return carry

        lax.fori_loop(0, CHUNKS, body, 0)

        @pl.when(has_up)
        def _():
            y_copy(0, c).start()

        @pl.when(has_down)
        def _():
            y_copy(1, c).start()

    def z_rows(m, get, put):
        for j in range(CHUNKS):
            value = get(j)
            head = value.astype(BF16)
            hl[0:m, 128 * j : 128 * j + 128] = head
            hl[m : 2 * m, 128 * j : 128 * j + 128] = (value - head.astype(F32)).astype(BF16)
        for k in range(CHUNKS // 2):
            start, kind = WINDOW_START[k], WINDOW_KIND[k]
            both = jnp.dot(
                hl[0 : 2 * m, start : start + 512], wv[kind, 0], preferred_element_type=F32
            )
            rest = jnp.dot(hl[0:m, start : start + 512], wv[kind, 1], preferred_element_type=F32)
            out = both[:m] + (both[m:] + rest)
            put(k, out[:, :128])
            put(CHUNKS // 2 + k, out[:, 128:])

    def z_tiles(c, first, step, count=2):
        def body(t, carry):
            base = pl.multiple_of((first + step * t) * TILE, TILE)

            def put(j, value):
                b_buf[c, j, pl.ds(base, TILE), :] = value

            z_rows(TILE, lambda j: cells[c][j, pl.ds(base, TILE), :], put)
            return carry

        lax.fori_loop(0, count, body, 0)

    def y_arrived(c):
        @pl.when(has_up)
        def _():
            y_copy(1, c).wait_recv()

        @pl.when(has_down)
        def _():
            y_copy(0, c).wait_recv()

    def z_halo(c):
        def put(j, value):
            yz[c, j] = value

        z_rows(
            4 * PLANES,
            lambda j: jnp.concatenate([yr[0, c, j], yr[1, c, j]], 0),
            put,
        )

    half = ROWS // 2
    row_at = lax.broadcasted_iota(jnp.int32, (half, 128), 0)

    def following(value, last):
        return jnp.where(row_at == half - 1, last, pltpu.roll(value, half - 1, 0))

    def preceding(value, first):
        return jnp.where(row_at == 0, first, pltpu.roll(value, 1, 0))

    def y_plane(c, p, j):
        base = pl.multiple_of(p * ROWS, ROWS)
        s, d = y_rows(c, j, base, [yz[c, j, pl.ds(PLANES * kind + p, 1), :] for kind in range(4)])
        cells[c][j, pl.ds(base, half), :] = s
        cells[c][j, pl.ds(base + half, half), :] = d

    def y_rows(c, j, base, rim):
        s = b_buf[c, j, pl.ds(base, half, stride=2), :]
        d = b_buf[c, j, pl.ds(base + 1, half, stride=2), :]
        pv, qv, sv, dv = rim
        d = d + pa * (s + following(s, sv))
        dm = pv + pa * s[0:1]
        s = s + ub * (preceding(d, dm) + d)
        sn = sv + ub * (d[half - 1 :] + dv)
        sm = qv + ub * dm
        dm = dm + pg * (sm + s[0:1])
        d = d + pg * (s + following(s, sn))
        s = s + ue * (preceding(d, dm) + d)
        return s, d

    def y_planes(c, starts):
        for start in starts:
            def body(q, carry):
                for j in range(CHUNKS):
                    y_plane(c, start + q, j)
                return carry

            lax.fori_loop(0, 4, body, 0)

    parts = ((0, 4, 0, half), (4, 4, 0, half), (0, 8, half, half), (0, 8, 0, ROWS))

    def x_copy(side, c, part):
        j0, jn, r0, rn = parts[part]
        place = (c, slice(None), pl.ds(j0, jn), pl.ds(r0, rn), slice(None))
        return pltpu.make_async_remote_copy(
            src_ref=xs.at[(side, *place)],
            dst_ref=xr.at[(1 - side, *place)],
            send_sem=x_send.at[side, c, part],
            recv_sem=x_recv.at[1 - side, c, part],
            device_id={"wide": left if side == 0 else right},
            device_id_type=MESH,
        )

    def x_values(c):
        def body(j, carry):
            def plane(p):
                return cells[c][j, p * ROWS : p * ROWS + ROWS, :]

            p0 = plane(0)
            xs[0, c, 0, j] = p0
            xs[0, c, 1, j] = plane(1) + pa * (p0 + plane(2))
            e2 = plane(PLANES - 2)
            xs[1, c, 0, j] = plane(PLANES - 1) + pa * e2
            xs[1, c, 1, j] = e2 + ub * (plane(PLANES - 3) + pa * (plane(PLANES - 4) + e2))
            return carry

        lax.fori_loop(0, CHUNKS, body, 0)

    def x_ends(c):
        def body(j, carry):

            def plane(p):
                return cells[c][j, p * ROWS : p * ROWS + ROWS, :]

            @pl.when(jnp.logical_not(has_left))
            def _():
                xr[0, c, 0, j] = plane(1) + pa * plane(2)
                xr[0, c, 1, j] = plane(2) + ub * (plane(3) + pa * (plane(2) + plane(4)))

            @pl.when(jnp.logical_not(has_right))
            def _():
                xr[1, c, 0, j] = plane(PLANES - 2)
                xr[1, c, 1, j] = plane(PLANES - 3) + pa * (plane(PLANES - 4) + plane(PLANES - 2))

            return carry

        lax.fori_loop(0, CHUNKS, body, 0)

    def x_start(c, part):
        @pl.when(has_left)
        def _():
            x_copy(0, c, part).start()

        @pl.when(has_right)
        def _():
            x_copy(1, c, part).start()

    def x_arrived(c, part):
        @pl.when(has_left)
        def _():
            x_copy(1, c, part).wait_recv()

        @pl.when(has_right)
        def _():
            x_copy(0, c, part).wait_recv()

    def m_copy(side):
        return pltpu.make_async_remote_copy(
            src_ref=ms.at[side],
            dst_ref=mr.at[1 - side],
            send_sem=m_send.at[side],
            recv_sem=m_recv.at[1 - side],
            device_id={"wide": left if side == 0 else right},
            device_id_type=MESH,
        )

    def m_values():
        def body(j, carry):
            for kind in range(4):
                def row(p):
                    return yr[kind // 2, 0, j, pl.ds(PLANES * (kind % 2) + p, 1), :]

                e2 = row(PLANES - 2)
                ms[0, j, kind : kind + 1, :] = row(0)
                ms[0, j, 4 + kind : 5 + kind, :] = row(1) + pa * (row(0) + row(2))
                ms[1, j, kind : kind + 1, :] = row(PLANES - 1) + pa * e2
                ms[1, j, 4 + kind : 5 + kind, :] = e2 + ub * (
                    row(PLANES - 3) + pa * (row(PLANES - 4) + e2)
                )
            return carry

        lax.fori_loop(0, CHUNKS, body, 0)

        @pl.when(has_left)
        def _():
            m_copy(0).start()

        @pl.when(has_right)
        def _():
            m_copy(1).start()

    def m_lift():
        x_arrived(0, 3)

        @pl.when(has_left)
        def _():
            m_copy(1).wait_recv()

        @pl.when(has_right)
        def _():
            m_copy(0).wait_recv()

        def get(j):
            return jnp.concatenate(
                [xr[0, 0, 0, j], xr[0, 0, 1, j], xr[1, 0, 0, j], xr[1, 0, 1, j], mr[0, j], mr[1, j]], 0
            )

        def put(j, value):
            b_buf[0, j, 0 : TILE + 16, :] = value

        z_rows(TILE + 16, get, put)

        def side_lift(side):
            def body(j, carry):
                for combo in range(2):
                    at = TILE + 8 * side + 4 * combo
                    s, d = y_rows(
                        0, j, ROWS * (2 * side + combo),
                        [b_buf[0, j, at + kind : at + kind + 1, :] for kind in range(4)],
                    )
                    xr[side, 0, combo, j, 0:half, :] = s
                    xr[side, 0, combo, j, half:, :] = d
                return carry

            lax.fori_loop(0, CHUNKS, body, 0)

        @pl.when(has_left)
        def _():
            side_lift(0)

        @pl.when(has_right)
        def _():
            side_lift(1)

    def x_lift(c, by, bz):
        def low_put(k, t, i, value):
            lll[k, pl.ds(pl.multiple_of(half * i + 8 * t, 8), 8), :] = value

        def put(band, i, rows, lanes, value):
            det_ref[c, band - 1, i, rows, lanes] = value

        x_lift_quarter(cells[c], xr, e_ref, c, by, bz, put, low_put)

    lane = lax.broadcasted_iota(jnp.int32, (8, 128), 1)
    low_half = lane < 64
    low_quarter = lax.rem(lane, 64) < 32

    xpos, zpos = wid // 4, lax.rem(wid, 4)

    def across(c, off, source):
        peer = lax.rem(xpos + off, 4)
        return pltpu.make_async_remote_copy(
            src_ref=lsend.at[pl.ds(4 * peer, 4), c],
            dst_ref=lmid.at[c, :, :, source],
            send_sem=l_send.at[0, c, off - 1],
            recv_sem=l_recv.at[0, c, source],
            device_id={"wide": 4 * peer + zpos},
            device_id_type=MESH,
        )

    def along(c, off, source):
        peer = lax.rem(zpos + off, 4)
        return pltpu.make_async_remote_copy(
            src_ref=lmid.at[c, peer],
            dst_ref=lrecv.at[c, :, :, source],
            send_sem=l_send.at[1, c, off - 1],
            recv_sem=l_recv.at[1, c, source],
            device_id={"wide": 4 * xpos + peer},
            device_id_type=MESH,
        )

    def l_pack(c):
        def body(k, carry):
            for g in range(8):
                v = [lll[k, pl.ds(4 * g + y, 8, stride=half), :] for y in range(4)]
                for a, b in ((0, 2), (1, 3)):
                    v[a], v[b] = (
                        jnp.where(low_half, v[a], pltpu.roll(v[b], 64, 1)),
                        jnp.where(low_half, pltpu.roll(v[a], 64, 1), v[b]),
                    )
                for a, b in ((0, 1), (2, 3)):
                    v[a], v[b] = (
                        jnp.where(low_quarter, v[a], pltpu.roll(v[b], 32, 1)),
                        jnp.where(low_quarter, pltpu.roll(v[a], 96, 1), v[b]),
                    )
                for y in range(4):
                    lsend[4 * k + y, c, g] = v[y]
            return carry

        lax.fori_loop(0, 4, body, 0)

        for off in (2, 1, 3):
            across(c, off, xpos).start()

        def own(z, carry):
            lmid[c, z, :, xpos] = lsend[4 * xpos + z, c]
            return carry

        lax.fori_loop(0, 4, own, 0)

    def l_turn(c):
        for off in (2, 1, 3):
            across(c, off, lax.rem(xpos + off, 4)).wait_recv()
        for off in (2, 1, 3):
            along(c, off, zpos).start()
        lrecv[c, :, :, zpos] = lmid[c, zpos]

    def l_arrived(c):
        for off in (2, 1, 3):
            along(c, off, lax.rem(zpos + off, 4)).wait_recv()

    def l_take(c):
        l_arrived(c)

        def put(rows, value):
            ap_ref[c, rows, :] = value

        turn_blocks(lrecv, c, put)

    loaded(0)
    x_values(0)
    x_start(0, 3)
    loaded(1)
    y_values(1)
    y_values(0)
    load_w.wait()
    z_tiles(1, 0, 3)
    loaded(2)
    y_values(2)
    y_arrived(1)
    z_halo(1)
    y_planes(1, (0, 12))
    x_values(1)
    x_start(1, 0)
    x_start(1, 1)
    y_arrived(0)
    m_values()
    z_tiles(2, 0, 3)
    y_arrived(2)
    z_halo(2)
    y_planes(2, (0, 12))
    x_values(2)
    x_start(2, 0)
    x_start(2, 1)
    z_tiles(0, 0, 1, 4)
    z_halo(0)
    y_planes(0, (0, 4, 8, 12))
    m_lift()
    x_ends(0)
    x_lift(0, 0, 0)
    l_pack(0)
    x_start(1, 2)
    x_lift(0, 0, 1)
    z_tiles(1, 1, 1)
    y_planes(1, (4, 8))
    l_turn(0)
    x_ends(1)
    x_arrived(1, 0)
    x_lift(1, 0, 0)
    l_pack(1)
    z_tiles(2, 1, 1)
    y_planes(2, (4, 8))
    l_turn(1)
    x_start(2, 2)
    x_ends(2)
    x_arrived(2, 0)
    x_lift(2, 0, 0)
    l_pack(2)
    x_lift(0, 1, 0)
    l_turn(2)
    x_lift(0, 1, 1)
    for c in (1, 2):
        x_arrived(c, 1)
        x_lift(c, 0, 1)
    x_arrived(1, 2)
    x_lift(1, 1, 0)
    x_lift(1, 1, 1)
    l_take(0)
    l_take(1)
    x_arrived(2, 2)
    l_arrived(2)

    for c in range(COMPS):
        @pl.when(has_up)
        def _():
            y_copy(0, c).wait_send()

        @pl.when(has_down)
        def _():
            y_copy(1, c).wait_send()

        for part in (range(3) if c else (3,)):
            @pl.when(has_left)
            def _():
                x_copy(0, c, part).wait_send()

            @pl.when(has_right)
            def _():
                x_copy(1, c, part).wait_send()

        if c == 0:
            @pl.when(has_left)
            def _():
                m_copy(0).wait_send()

            @pl.when(has_right)
            def _():
                m_copy(1).wait_send()

        for off in (1, 2, 3):
            across(c, off, xpos).wait_send()
            along(c, off, zpos).wait_send()


def finish(
    e_ref, cells, rims, received, approx, details, approx_out, details_out,
    last_details, last_approx, approx_sem, details_sem,
):
    c = COMPS - 1
    bands = (2, 3, 6, 7)
    early, late = [], {}
    for comp in range(COMPS):
        for band in range(1, 8):
            mine = comp == c and band in bands
            source = last_details.at[bands.index(band)] if mine else details.at[comp, band - 1]
            copy = pltpu.make_async_copy(
                source, details_out.at[comp, band - 1], details_sem.at[comp, band - 1]
            )
            if mine:
                late[band] = copy
            else:
                early.append(copy)
        copy = pltpu.make_async_copy(
            last_approx if comp == c else approx.at[comp], approx_out.at[comp], approx_sem.at[comp]
        )
        if comp == c:
            late[0] = copy
        else:
            early.append(copy)
    for copy in early:
        copy.start()

    def put(band, i, rows, lanes, value):
        last_details[bands.index(band), i, rows, lanes] = value

    for bz in range(2):
        x_lift_quarter(cells, rims, e_ref, c, 1, bz, put, None)
        late[2 + bz].start()
        late[6 + bz].start()

    def put_block(rows, value):
        last_approx[rows, :] = value

    turn_blocks(received, c, put_block)
    late[0].start()
    for copy in early + list(late.values()):
        copy.wait()


def local(n_narrow, n_wide, velocity, exponents):
    cells = velocity.reshape((COMPS, PLANES * ROWS, DEPTH))
    approx, details, last, rims, received = pl.pallas_call(
        functools.partial(kernel, n_narrow, n_wide),
        out_shape=(
            pltpu.VMEM((COMPS - 1, 1024, 128), F32),
            pltpu.VMEM((COMPS, 7, PLANES // 2, ROWS // 2, DEPTH // 2), F32),
            pltpu.VMEM((CHUNKS, PLANES * ROWS, 128), F32),
            pltpu.VMEM((2, COMPS, 2, CHUNKS, ROWS, 128), F32),
            pltpu.VMEM((COMPS, 8, 4, 4, 8, 128), F32),
        ),
        in_specs=[
            pl.BlockSpec(memory_space=pl.ANY),
            pl.BlockSpec(memory_space=pltpu.SMEM),
            pl.BlockSpec(memory_space=pl.ANY),
        ],
        out_specs=(pl.BlockSpec(memory_space=pltpu.VMEM),) * 5,
        scratch_shapes=[
            pltpu.VMEM((CHUNKS, PLANES * ROWS, 128), F32),
            pltpu.VMEM((CHUNKS, PLANES * ROWS, 128), F32),
            pltpu.VMEM((COMPS, CHUNKS, PLANES * ROWS, 128), F32),
            pltpu.VMEM((2 * TILE + 32, DEPTH), BF16),
            pltpu.VMEM((3, 2, 512, 256), BF16),
            pltpu.VMEM((2, COMPS, CHUNKS, 2 * PLANES, 128), F32),
            pltpu.VMEM((2, COMPS, CHUNKS, 2 * PLANES, 128), F32),
            pltpu.VMEM((COMPS, CHUNKS, 4 * PLANES, 128), F32),
            pltpu.VMEM((2, COMPS, 2, CHUNKS, ROWS, 128), F32),
            pltpu.VMEM((2, CHUNKS, 8, 128), F32),
            pltpu.VMEM((2, CHUNKS, 8, 128), F32),
            pltpu.VMEM((4, 256, 128), F32),
            pltpu.VMEM((16, COMPS, 8, 8, 128), F32),
            pltpu.VMEM((COMPS, 4, 8, 4, 8, 128), F32),
            pltpu.SemaphoreType.DMA((COMPS, CHUNKS)),
            pltpu.SemaphoreType.DMA,
            pltpu.SemaphoreType.DMA((2, COMPS)),
            pltpu.SemaphoreType.DMA((2, COMPS)),
            pltpu.SemaphoreType.DMA((2, COMPS, 4)),
            pltpu.SemaphoreType.DMA((2, COMPS, 4)),
            pltpu.SemaphoreType.DMA((2,)),
            pltpu.SemaphoreType.DMA((2,)),
            pltpu.SemaphoreType.DMA((2, COMPS, 3)),
            pltpu.SemaphoreType.DMA((2, COMPS, 4)),
        ],
        compiler_params=pltpu.CompilerParams(
            collective_id=0, has_side_effects=True, vmem_limit_bytes=38 * 1024 * 1024
        ),
        cost_estimate=pl.CostEstimate(
            flops=10_000_000_000, bytes_accessed=26_000_000, transcendentals=0
        ),
    )(cells, exponents, jnp.asarray(z_weights()))
    approx, details = pl.pallas_call(
        finish,
        out_shape=(
            jax.ShapeDtypeStruct((COMPS, 1024, 128), F32),
            jax.ShapeDtypeStruct(details.shape, F32),
        ),
        in_specs=[pl.BlockSpec(memory_space=pltpu.SMEM)]
        + [pl.BlockSpec(memory_space=pltpu.VMEM)] * 3
        + [pl.BlockSpec(memory_space=pl.ANY)] * 2,
        out_specs=(pl.BlockSpec(memory_space=pl.ANY),) * 2,
        scratch_shapes=[
            pltpu.VMEM((4, PLANES // 2, ROWS // 2, DEPTH // 2), F32),
            pltpu.VMEM((1024, 128), F32),
            pltpu.SemaphoreType.DMA((COMPS,)),
            pltpu.SemaphoreType.DMA((COMPS, 7)),
        ],
        compiler_params=pltpu.CompilerParams(vmem_limit_bytes=4 * 1024 * 1024),
    )(exponents, last, rims, received, approx, details)
    approx = approx.reshape((COMPS, ROWS // 2, 32, 128))
    return jnp.transpose(approx, (0, 3, 1, 2)), details


def solution(mesh):
    placed = (P(None, "wide", "narrow", None), P())
    return jax.shard_map(
        functools.partial(local, mesh.shape["narrow"], mesh.shape["wide"]),
        mesh=mesh,
        in_specs=placed,
        out_specs=(P(None, None, "narrow", "wide"), P(None, None, "wide", "narrow", None)),
        check_vma=False,
    )
```

```python
import functools

import jax
import jax.numpy as jnp
import ml_dtypes
import numpy as np
from jax import lax
from jax.experimental import pallas as pl
from jax.experimental.pallas import tpu as pltpu
from jax.sharding import PartitionSpec as P

MESH = pl.DeviceIdType.MESH
F32 = jnp.float32
BF16 = jnp.bfloat16

pa = -1.586134342
ub = -0.05298011854
pg = 0.8829110762
ue = 0.4435068522
scaling = 1.149604398

COMPS = 3
PLANES = 16
ROWS = 64
DEPTH = 1024
CHUNKS = DEPTH // 128
TILE = 256
WINDOW_START = (0, 128, 384, 512)
WINDOW_KIND = (0, 1, 1, 2)


def z_weights():
    ext = np.pad(np.eye(DEPTH), ((0, 0), (4, 4)), mode="reflect")
    s, d = ext[:, 0::2], ext[:, 1::2]
    d = d[:, :-1] + pa * (s[:, :-1] + s[:, 1:])
    s = s[:, 1:-1] + ub * (d[:, :-1] + d[:, 1:])
    d = d[:, 1:-1] + pg * (s[:, :-1] + s[:, 1:])
    s = s[:, 1:-1] + ue * (d[:, :-1] + d[:, 1:])
    low, high = s * scaling, d[:, 1:] / scaling
    kinds = []
    for k in (0, 1, 3):
        rows = slice(WINDOW_START[k], WINDOW_START[k] + 512)
        cols = slice(128 * k, 128 * k + 128)
        kinds.append(np.concatenate([low[rows, cols], high[rows, cols]], 1))
    full = np.stack(kinds)
    head = full.astype(np.float32).astype(ml_dtypes.bfloat16)
    rest = (full - head.astype(np.float64)).astype(np.float32).astype(ml_dtypes.bfloat16)
    return np.stack([head, rest], 1)


def factor(e_ref, band):
    shift = lax.shift_left(jnp.int32(1), 15 - e_ref[band - 1]).astype(F32)
    ups = 2 - 2 * (band // 4) - 2 * ((band // 2) % 2)
    return shift * (2.0**-15 * scaling**ups)


def x_lift_quarter(cells, rims, e_ref, c, by, bz, put, low_put):
    half = ROWS // 2
    low_band, high_band = 2 * by + bz, 4 + 2 * by + bz
    high_scale = factor(e_ref, high_band)
    low_scale = factor(e_ref, low_band) if low_band else None

    def body(at, carry):
        k, t = at // 4, lax.rem(at, 4)
        j = 4 * bz + k
        row = pl.multiple_of(half * by + 8 * t, 8)

        def plane(p):
            return cells[j, pl.ds(pl.multiple_of(p * ROWS + row, 8), 8), :]

        s = [plane(2 * i) for i in range(8)]
        d = [plane(2 * i + 1) for i in range(8)]
        pv = rims[0, c, 0, j, pl.ds(row, 8), :]
        qv = rims[0, c, 1, j, pl.ds(row, 8), :]
        sv = rims[1, c, 0, j, pl.ds(row, 8), :]
        dv = rims[1, c, 1, j, pl.ds(row, 8), :]
        s.append(sv)
        d = [d[i] + pa * (s[i] + s[i + 1]) for i in range(8)]
        dm = pv + pa * s[0]
        sn = sv + ub * (d[7] + dv)
        sm = qv + ub * dm
        s = [s[i] + ub * ((d[i - 1] if i else dm) + d[i]) for i in range(8)]
        dm = dm + pg * (sm + s[0])
        s.append(sn)
        d = [d[i] + pg * (s[i] + s[i + 1]) for i in range(8)]
        s = [s[i] + ue * ((d[i - 1] if i else dm) + d[i]) for i in range(8)]
        lanes = pl.ds(pl.multiple_of(128 * k, 128), 128)
        rows = pl.ds(pl.multiple_of(8 * t, 8), 8)
        for i in range(8):
            v = d[i] * high_scale
            put(high_band, i, rows, lanes, v - jnp.clip(v, -0.5, 0.5))
            if low_band:
                v = s[i] * low_scale
                put(low_band, i, rows, lanes, v - jnp.clip(v, -0.5, 0.5))
            else:
                low_put(k, t, i, s[i] * (scaling * scaling))
        return carry

    lax.fori_loop(0, 16, body, 0)


def turn_blocks(received, c, put):
    def body(g, carry):
        put(pl.ds(pl.multiple_of(128 * g, 128), 128), received[c, g].reshape((128, 128)).T)
        return carry

    lax.fori_loop(0, 8, body, 0)


def kernel(
    n_narrow, n_wide,
    x_ref, e_ref, w_ref, ap_ref, det_ref, a_last, xr, lrecv,
    a_first, a_second, b_buf, hl, wv, ys, yr, yz, xs, ms, mr, lll, lsend, lmid,
    load_sem, outer_sem, w_sem, y_send, y_recv, x_send, x_recv, m_send, m_recv, l_send, l_recv,
):
    cells = (a_first, a_second, a_last)
    nar = lax.axis_index("narrow")
    wid = lax.axis_index("wide")
    up = lax.rem(nar + n_narrow - 1, n_narrow)
    down = lax.rem(nar + 1, n_narrow)
    left = lax.rem(wid + n_wide - 1, n_wide)
    right = lax.rem(wid + 1, n_wide)
    has_up, has_down = nar > 0, nar < n_narrow - 1
    has_left, has_right = wid > 0, wid < n_wide - 1

    def load(c, j):
        return pltpu.make_async_copy(
            x_ref.at[c, :, pl.ds(128 * j, 128)], cells[c].at[j], load_sem.at[c, j]
        )

    def load_outer(side, j):
        rows = pl.ds(3 * TILE * side, TILE)
        return pltpu.make_async_copy(
            x_ref.at[0, rows, pl.ds(128 * j, 128)], cells[0].at[j, rows], outer_sem.at[side, j]
        )

    def load_inner(j):
        rows = pl.ds(TILE, 2 * TILE)
        return pltpu.make_async_copy(
            x_ref.at[0, rows, pl.ds(128 * j, 128)], cells[0].at[j, rows], load_sem.at[0, j]
        )

    load_w = pltpu.make_async_copy(w_ref, wv, w_sem)
    for j in range(CHUNKS):
        load_outer(0, j).start()
        load_outer(1, j).start()
    for j in range(CHUNKS):
        load_inner(j).start()

    barrier = pltpu.get_barrier_semaphore()

    def greet(off, carry):
        for peer in (
            4 * lax.rem(wid // 4 + off, 4) + lax.rem(wid, 4),
            4 * (wid // 4) + lax.rem(wid + off, 4),
        ):
            pl.semaphore_signal(barrier, inc=1, device_id={"wide": peer}, device_id_type=MESH)
        return carry

    lax.fori_loop(1, 4, greet, 0)
    turn_left = jnp.logical_and(lax.rem(wid, 4) == 0, has_left)
    turn_right = jnp.logical_and(lax.rem(wid, 4) == 3, has_right)

    @pl.when(turn_left)
    def _():
        pl.semaphore_signal(barrier, inc=1, device_id={"wide": left}, device_id_type=MESH)

    @pl.when(turn_right)
    def _():
        pl.semaphore_signal(barrier, inc=1, device_id={"wide": right}, device_id_type=MESH)

    @pl.when(has_up)
    def _():
        pl.semaphore_signal(barrier, inc=1, device_id={"narrow": up}, device_id_type=MESH)

    @pl.when(has_down)
    def _():
        pl.semaphore_signal(barrier, inc=1, device_id={"narrow": down}, device_id_type=MESH)

    pl.semaphore_wait(
        barrier,
        6
        + turn_left.astype(jnp.int32)
        + turn_right.astype(jnp.int32)
        + has_up.astype(jnp.int32)
        + has_down.astype(jnp.int32),
    )

    def y_copy(side, c):
        return pltpu.make_async_remote_copy(
            src_ref=ys.at[side, c],
            dst_ref=yr.at[1 - side, c],
            send_sem=y_send.at[side, c],
            recv_sem=y_recv.at[1 - side, c],
            device_id={"narrow": up if side == 0 else down},
            device_id_type=MESH,
        )

    def loaded(c):
        for j in range(CHUNKS):
            (load(c, j) if c else load_inner(j)).wait()
        if c + 1 < COMPS:
            for j in range(CHUNKS):
                load(c + 1, j).start()

    def y_values(c):
        def body(j, carry):
            def row(r):
                return cells[c][j, pl.ds(r, PLANES, stride=ROWS), :]

            r0, r1, r2 = row(0), row(1), row(2)
            e0, e1, e2, e3 = row(ROWS - 4), row(ROWS - 3), row(ROWS - 2), row(ROWS - 1)
            before_last = e1 + pa * (e0 + e2)
            ys[0, c, j, 0:PLANES, :] = r0
            ys[0, c, j, PLANES:, :] = r1 + pa * (r0 + r2)
            ys[1, c, j, 0:PLANES, :] = e3 + pa * e2
            ys[1, c, j, PLANES:, :] = e2 + ub * before_last

            @pl.when(jnp.logical_not(has_up))
            def _():
                r3, r4 = row(3), row(4)
                yr[0, c, j, 0:PLANES, :] = r1 + pa * r2
                yr[0, c, j, PLANES:, :] = r2 + ub * (r3 + pa * (r2 + r4))

            @pl.when(jnp.logical_not(has_down))
            def _():
                yr[1, c, j, 0:PLANES, :] = e2
                yr[1, c, j, PLANES:, :] = before_last

            return carry

        lax.fori_loop(0, CHUNKS, body, 0)

        @pl.when(has_up)
        def _():
            y_copy(0, c).start()

        @pl.when(has_down)
        def _():
            y_copy(1, c).start()

    def z_rows(m, get, put):
        for j in range(CHUNKS):
            value = get(j)
            head = value.astype(BF16)
            hl[0:m, 128 * j : 128 * j + 128] = head
            hl[m : 2 * m, 128 * j : 128 * j + 128] = (value - head.astype(F32)).astype(BF16)
        for k in range(CHUNKS // 2):
            start, kind = WINDOW_START[k], WINDOW_KIND[k]
            both = jnp.dot(
                hl[0 : 2 * m, start : start + 512], wv[kind, 0], preferred_element_type=F32
            )
            rest = jnp.dot(hl[0:m, start : start + 512], wv[kind, 1], preferred_element_type=F32)
            out = both[:m] + (both[m:] + rest)
            put(k, out[:, :128])
            put(CHUNKS // 2 + k, out[:, 128:])

    def z_tiles(c, first, step, count=2):
        def body(t, carry):
            base = pl.multiple_of((first + step * t) * TILE, TILE)

            def put(j, value):
                b_buf[c, j, pl.ds(base, TILE), :] = value

            z_rows(TILE, lambda j: cells[c][j, pl.ds(base, TILE), :], put)
            return carry

        lax.fori_loop(0, count, body, 0)

    def y_arrived(c):
        @pl.when(has_up)
        def _():
            y_copy(1, c).wait_recv()

        @pl.when(has_down)
        def _():
            y_copy(0, c).wait_recv()

    def z_halo(c):
        def put(j, value):
            yz[c, j] = value

        z_rows(
            4 * PLANES,
            lambda j: jnp.concatenate([yr[0, c, j], yr[1, c, j]], 0),
            put,
        )

    half = ROWS // 2
    row_at = lax.broadcasted_iota(jnp.int32, (half, 128), 0)

    def following(value, last):
        return jnp.where(row_at == half - 1, last, pltpu.roll(value, half - 1, 0))

    def preceding(value, first):
        return jnp.where(row_at == 0, first, pltpu.roll(value, 1, 0))

    def y_plane(c, p, j):
        base = pl.multiple_of(p * ROWS, ROWS)
        s, d = y_rows(c, j, base, [yz[c, j, pl.ds(PLANES * kind + p, 1), :] for kind in range(4)])
        cells[c][j, pl.ds(base, half), :] = s
        cells[c][j, pl.ds(base + half, half), :] = d

    def y_rows(c, j, base, rim):
        s = b_buf[c, j, pl.ds(base, half, stride=2), :]
        d = b_buf[c, j, pl.ds(base + 1, half, stride=2), :]
        pv, qv, sv, dv = rim
        d = d + pa * (s + following(s, sv))
        dm = pv + pa * s[0:1]
        s = s + ub * (preceding(d, dm) + d)
        sn = sv + ub * (d[half - 1 :] + dv)
        sm = qv + ub * dm
        dm = dm + pg * (sm + s[0:1])
        d = d + pg * (s + following(s, sn))
        s = s + ue * (preceding(d, dm) + d)
        return s, d

    def y_planes(c, starts):
        for start in starts:
            def body(q, carry):
                for j in range(CHUNKS):
                    y_plane(c, start + q, j)
                return carry

            lax.fori_loop(0, 4, body, 0)

    parts = ((0, 4, 0, half), (4, 4, 0, half), (0, 8, half, half), (0, 8, 0, ROWS))

    def x_copy(side, c, part):
        j0, jn, r0, rn = parts[part]
        place = (c, slice(None), pl.ds(j0, jn), pl.ds(r0, rn), slice(None))
        return pltpu.make_async_remote_copy(
            src_ref=xs.at[(side, *place)],
            dst_ref=xr.at[(1 - side, *place)],
            send_sem=x_send.at[side, c, part],
            recv_sem=x_recv.at[1 - side, c, part],
            device_id={"wide": left if side == 0 else right},
            device_id_type=MESH,
        )

    def x_values(c):
        def body(j, carry):
            def plane(p):
                return cells[c][j, p * ROWS : p * ROWS + ROWS, :]

            p0 = plane(0)
            xs[0, c, 0, j] = p0
            xs[0, c, 1, j] = plane(1) + pa * (p0 + plane(2))
            e2 = plane(PLANES - 2)
            xs[1, c, 0, j] = plane(PLANES - 1) + pa * e2
            xs[1, c, 1, j] = e2 + ub * (plane(PLANES - 3) + pa * (plane(PLANES - 4) + e2))
            return carry

        lax.fori_loop(0, CHUNKS, body, 0)

    def x_ends(c):
        def body(j, carry):

            def plane(p):
                return cells[c][j, p * ROWS : p * ROWS + ROWS, :]

            @pl.when(jnp.logical_not(has_left))
            def _():
                xr[0, c, 0, j] = plane(1) + pa * plane(2)
                xr[0, c, 1, j] = plane(2) + ub * (plane(3) + pa * (plane(2) + plane(4)))

            @pl.when(jnp.logical_not(has_right))
            def _():
                xr[1, c, 0, j] = plane(PLANES - 2)
                xr[1, c, 1, j] = plane(PLANES - 3) + pa * (plane(PLANES - 4) + plane(PLANES - 2))

            return carry

        lax.fori_loop(0, CHUNKS, body, 0)

    def x_start(c, part):
        @pl.when(has_left)
        def _():
            x_copy(0, c, part).start()

        @pl.when(has_right)
        def _():
            x_copy(1, c, part).start()

    def x_arrived(c, part):
        @pl.when(has_left)
        def _():
            x_copy(1, c, part).wait_recv()

        @pl.when(has_right)
        def _():
            x_copy(0, c, part).wait_recv()

    def m_copy(side):
        return pltpu.make_async_remote_copy(
            src_ref=ms.at[side],
            dst_ref=mr.at[1 - side],
            send_sem=m_send.at[side],
            recv_sem=m_recv.at[1 - side],
            device_id={"wide": left if side == 0 else right},
            device_id_type=MESH,
        )

    def m_values():
        def body(j, carry):
            for kind in range(4):
                def row(p):
                    return yr[kind // 2, 0, j, pl.ds(PLANES * (kind % 2) + p, 1), :]

                e2 = row(PLANES - 2)
                ms[0, j, kind : kind + 1, :] = row(0)
                ms[0, j, 4 + kind : 5 + kind, :] = row(1) + pa * (row(0) + row(2))
                ms[1, j, kind : kind + 1, :] = row(PLANES - 1) + pa * e2
                ms[1, j, 4 + kind : 5 + kind, :] = e2 + ub * (
                    row(PLANES - 3) + pa * (row(PLANES - 4) + e2)
                )
            return carry

        lax.fori_loop(0, CHUNKS, body, 0)

        @pl.when(has_left)
        def _():
            m_copy(0).start()

        @pl.when(has_right)
        def _():
            m_copy(1).start()

    def m_lift():
        x_arrived(0, 3)

        @pl.when(has_left)
        def _():
            m_copy(1).wait_recv()

        @pl.when(has_right)
        def _():
            m_copy(0).wait_recv()

        def get(j):
            return jnp.concatenate(
                [xr[0, 0, 0, j], xr[0, 0, 1, j], xr[1, 0, 0, j], xr[1, 0, 1, j], mr[0, j], mr[1, j]], 0
            )

        def put(j, value):
            b_buf[0, j, 0 : TILE + 16, :] = value

        z_rows(TILE + 16, get, put)

        def side_lift(side):
            def body(j, carry):
                for combo in range(2):
                    at = TILE + 8 * side + 4 * combo
                    s, d = y_rows(
                        0, j, ROWS * (2 * side + combo),
                        [b_buf[0, j, at + kind : at + kind + 1, :] for kind in range(4)],
                    )
                    xr[side, 0, combo, j, 0:half, :] = s
                    xr[side, 0, combo, j, half:, :] = d
                return carry

            lax.fori_loop(0, CHUNKS, body, 0)

        @pl.when(has_left)
        def _():
            side_lift(0)

        @pl.when(has_right)
        def _():
            side_lift(1)

    def x_lift(c, by, bz):
        def low_put(k, t, i, value):
            lll[k, pl.ds(pl.multiple_of(half * i + 8 * t, 8), 8), :] = value

        def put(band, i, rows, lanes, value):
            det_ref[c, band - 1, i, rows, lanes] = value

        x_lift_quarter(cells[c], xr, e_ref, c, by, bz, put, low_put)

    lane = lax.broadcasted_iota(jnp.int32, (8, 128), 1)
    low_half = lane < 64
    low_quarter = lax.rem(lane, 64) < 32

    xpos, zpos = wid // 4, lax.rem(wid, 4)

    def across(c, off, source):
        peer = lax.rem(xpos + off, 4)
        return pltpu.make_async_remote_copy(
            src_ref=lsend.at[pl.ds(4 * peer, 4), c],
            dst_ref=lmid.at[c, :, :, source],
            send_sem=l_send.at[0, c, off - 1],
            recv_sem=l_recv.at[0, c, source],
            device_id={"wide": 4 * peer + zpos},
            device_id_type=MESH,
        )

    def along(c, off, source):
        peer = lax.rem(zpos + off, 4)
        return pltpu.make_async_remote_copy(
            src_ref=lmid.at[c, peer],
            dst_ref=lrecv.at[c, :, :, source],
            send_sem=l_send.at[1, c, off - 1],
            recv_sem=l_recv.at[1, c, source],
            device_id={"wide": 4 * xpos + peer},
            device_id_type=MESH,
        )

    def l_pack(c):
        def body(k, carry):
            for g in range(8):
                v = [lll[k, pl.ds(4 * g + y, 8, stride=half), :] for y in range(4)]
                for a, b in ((0, 2), (1, 3)):
                    v[a], v[b] = (
                        jnp.where(low_half, v[a], pltpu.roll(v[b], 64, 1)),
                        jnp.where(low_half, pltpu.roll(v[a], 64, 1), v[b]),
                    )
                for a, b in ((0, 1), (2, 3)):
                    v[a], v[b] = (
                        jnp.where(low_quarter, v[a], pltpu.roll(v[b], 32, 1)),
                        jnp.where(low_quarter, pltpu.roll(v[a], 96, 1), v[b]),
                    )
                for y in range(4):
                    lsend[4 * k + y, c, g] = v[y]
            return carry

        lax.fori_loop(0, 4, body, 0)

        for off in (2, 1, 3):
            across(c, off, xpos).start()

        def own(z, carry):
            lmid[c, z, :, xpos] = lsend[4 * xpos + z, c]
            return carry

        lax.fori_loop(0, 4, own, 0)

    def l_turn(c):
        for off in (2, 1, 3):
            across(c, off, lax.rem(xpos + off, 4)).wait_recv()
        for off in (2, 1, 3):
            along(c, off, zpos).start()
        lrecv[c, :, :, zpos] = lmid[c, zpos]

    def l_arrived(c):
        for off in (2, 1, 3):
            along(c, off, lax.rem(zpos + off, 4)).wait_recv()

    def l_take(c):
        l_arrived(c)

        def put(rows, value):
            ap_ref[c, rows, :] = value

        turn_blocks(lrecv, c, put)

    for j in range(CHUNKS):
        load_outer(0, j).wait()
        load_outer(1, j).wait()
    x_values(0)
    x_start(0, 3)
    loaded(0)
    load_w.start()
    loaded(1)
    y_values(1)
    y_values(0)
    load_w.wait()
    z_tiles(1, 0, 3)
    loaded(2)
    y_values(2)
    y_arrived(1)
    z_halo(1)
    y_planes(1, (0, 12))
    x_values(1)
    x_start(1, 0)
    x_start(1, 1)
    y_arrived(0)
    m_values()
    z_tiles(2, 0, 3)
    y_arrived(2)
    z_halo(2)
    y_planes(2, (0, 12))
    x_values(2)
    x_start(2, 0)
    x_start(2, 1)
    z_tiles(0, 0, 1, 4)
    z_halo(0)
    y_planes(0, (0, 4, 8, 12))
    m_lift()
    x_ends(0)
    x_lift(0, 0, 0)
    l_pack(0)
    x_start(1, 2)
    x_lift(0, 0, 1)
    z_tiles(1, 1, 1)
    y_planes(1, (4, 8))
    l_turn(0)
    x_ends(1)
    x_arrived(1, 0)
    x_lift(1, 0, 0)
    l_pack(1)
    z_tiles(2, 1, 1)
    y_planes(2, (4, 8))
    l_turn(1)
    x_start(2, 2)
    x_ends(2)
    x_arrived(2, 0)
    x_lift(2, 0, 0)
    l_pack(2)
    x_lift(0, 1, 0)
    l_turn(2)
    x_lift(0, 1, 1)
    for c in (1, 2):
        x_arrived(c, 1)
        x_lift(c, 0, 1)
    x_arrived(1, 2)
    x_lift(1, 1, 0)
    x_lift(1, 1, 1)
    l_take(0)
    l_take(1)
    x_arrived(2, 2)
    l_arrived(2)

    for c in range(COMPS):
        @pl.when(has_up)
        def _():
            y_copy(0, c).wait_send()

        @pl.when(has_down)
        def _():
            y_copy(1, c).wait_send()

        for part in (range(3) if c else (3,)):
            @pl.when(has_left)
            def _():
                x_copy(0, c, part).wait_send()

            @pl.when(has_right)
            def _():
                x_copy(1, c, part).wait_send()

        if c == 0:
            @pl.when(has_left)
            def _():
                m_copy(0).wait_send()

            @pl.when(has_right)
            def _():
                m_copy(1).wait_send()

        for off in (1, 2, 3):
            across(c, off, xpos).wait_send()
            along(c, off, zpos).wait_send()


def finish(
    e_ref, cells, rims, received, approx, details, approx_out, details_out,
    last_details, last_approx, approx_sem, details_sem,
):
    c = COMPS - 1
    bands = (2, 3, 6, 7)
    early, late = [], {}
    for comp in range(COMPS):
        for band in range(1, 8):
            mine = comp == c and band in bands
            source = last_details.at[bands.index(band)] if mine else details.at[comp, band - 1]
            copy = pltpu.make_async_copy(
                source, details_out.at[comp, band - 1], details_sem.at[comp, band - 1]
            )
            if mine:
                late[band] = copy
            else:
                early.append(copy)
        copy = pltpu.make_async_copy(
            last_approx if comp == c else approx.at[comp], approx_out.at[comp], approx_sem.at[comp]
        )
        if comp == c:
            late[0] = copy
        else:
            early.append(copy)
    for copy in early:
        copy.start()

    def put(band, i, rows, lanes, value):
        last_details[bands.index(band), i, rows, lanes] = value

    for bz in range(2):
        x_lift_quarter(cells, rims, e_ref, c, 1, bz, put, None)
        late[2 + bz].start()
        late[6 + bz].start()

    def put_block(rows, value):
        last_approx[rows, :] = value

    turn_blocks(received, c, put_block)
    late[0].start()
    for copy in early + list(late.values()):
        copy.wait()


def local(n_narrow, n_wide, velocity, exponents):
    cells = velocity.reshape((COMPS, PLANES * ROWS, DEPTH))
    approx, details, last, rims, received = pl.pallas_call(
        functools.partial(kernel, n_narrow, n_wide),
        out_shape=(
            pltpu.VMEM((COMPS - 1, 1024, 128), F32),
            pltpu.VMEM((COMPS, 7, PLANES // 2, ROWS // 2, DEPTH // 2), F32),
            pltpu.VMEM((CHUNKS, PLANES * ROWS, 128), F32),
            pltpu.VMEM((2, COMPS, 2, CHUNKS, ROWS, 128), F32),
            pltpu.VMEM((COMPS, 8, 4, 4, 8, 128), F32),
        ),
        in_specs=[
            pl.BlockSpec(memory_space=pl.ANY),
            pl.BlockSpec(memory_space=pltpu.SMEM),
            pl.BlockSpec(memory_space=pl.ANY),
        ],
        out_specs=(pl.BlockSpec(memory_space=pltpu.VMEM),) * 5,
        scratch_shapes=[
            pltpu.VMEM((CHUNKS, PLANES * ROWS, 128), F32),
            pltpu.VMEM((CHUNKS, PLANES * ROWS, 128), F32),
            pltpu.VMEM((COMPS, CHUNKS, PLANES * ROWS, 128), F32),
            pltpu.VMEM((2 * TILE + 32, DEPTH), BF16),
            pltpu.VMEM((3, 2, 512, 256), BF16),
            pltpu.VMEM((2, COMPS, CHUNKS, 2 * PLANES, 128), F32),
            pltpu.VMEM((2, COMPS, CHUNKS, 2 * PLANES, 128), F32),
            pltpu.VMEM((COMPS, CHUNKS, 4 * PLANES, 128), F32),
            pltpu.VMEM((2, COMPS, 2, CHUNKS, ROWS, 128), F32),
            pltpu.VMEM((2, CHUNKS, 8, 128), F32),
            pltpu.VMEM((2, CHUNKS, 8, 128), F32),
            pltpu.VMEM((4, 256, 128), F32),
            pltpu.VMEM((16, COMPS, 8, 8, 128), F32),
            pltpu.VMEM((COMPS, 4, 8, 4, 8, 128), F32),
            pltpu.SemaphoreType.DMA((COMPS, CHUNKS)),
            pltpu.SemaphoreType.DMA((2, CHUNKS)),
            pltpu.SemaphoreType.DMA,
            pltpu.SemaphoreType.DMA((2, COMPS)),
            pltpu.SemaphoreType.DMA((2, COMPS)),
            pltpu.SemaphoreType.DMA((2, COMPS, 4)),
            pltpu.SemaphoreType.DMA((2, COMPS, 4)),
            pltpu.SemaphoreType.DMA((2,)),
            pltpu.SemaphoreType.DMA((2,)),
            pltpu.SemaphoreType.DMA((2, COMPS, 3)),
            pltpu.SemaphoreType.DMA((2, COMPS, 4)),
        ],
        compiler_params=pltpu.CompilerParams(
            collective_id=0, has_side_effects=True, vmem_limit_bytes=38 * 1024 * 1024
        ),
        cost_estimate=pl.CostEstimate(
            flops=10_000_000_000, bytes_accessed=26_000_000, transcendentals=0
        ),
    )(cells, exponents, jnp.asarray(z_weights()))
    approx, details = pl.pallas_call(
        finish,
        out_shape=(
            jax.ShapeDtypeStruct((COMPS, 1024, 128), F32),
            jax.ShapeDtypeStruct(details.shape, F32),
        ),
        in_specs=[pl.BlockSpec(memory_space=pltpu.SMEM)]
        + [pl.BlockSpec(memory_space=pltpu.VMEM)] * 3
        + [pl.BlockSpec(memory_space=pl.ANY)] * 2,
        out_specs=(pl.BlockSpec(memory_space=pl.ANY),) * 2,
        scratch_shapes=[
            pltpu.VMEM((4, PLANES // 2, ROWS // 2, DEPTH // 2), F32),
            pltpu.VMEM((1024, 128), F32),
            pltpu.SemaphoreType.DMA((COMPS,)),
            pltpu.SemaphoreType.DMA((COMPS, 7)),
        ],
        compiler_params=pltpu.CompilerParams(vmem_limit_bytes=4 * 1024 * 1024),
    )(exponents, last, rims, received, approx, details)
    approx = approx.reshape((COMPS, ROWS // 2, 32, 128))
    return jnp.transpose(approx, (0, 3, 1, 2)), details


def solution(mesh):
    placed = (P(None, "wide", "narrow", None), P())
    return jax.shard_map(
        functools.partial(local, mesh.shape["narrow"], mesh.shape["wide"]),
        mesh=mesh,
        in_specs=placed,
        out_specs=(P(None, None, "narrow", "wide"), P(None, None, "wide", "narrow", None)),
        check_vma=False,
    )
```

```python
import functools

import jax
import jax.numpy as jnp
import ml_dtypes
import numpy as np
from jax import lax
from jax.experimental import pallas as pl
from jax.experimental.pallas import tpu as pltpu
from jax.sharding import PartitionSpec as P

MESH = pl.DeviceIdType.MESH
F32 = jnp.float32
BF16 = jnp.bfloat16

pa = -1.586134342
ub = -0.05298011854
pg = 0.8829110762
ue = 0.4435068522
scaling = 1.149604398

COMPS = 3
PLANES = 16
ROWS = 64
DEPTH = 1024
CHUNKS = DEPTH // 128
TILE = 256
WINDOW_START = (0, 128, 384, 512)
WINDOW_KIND = (0, 1, 1, 2)


def z_weights():
    ext = np.pad(np.eye(DEPTH), ((0, 0), (4, 4)), mode="reflect")
    s, d = ext[:, 0::2], ext[:, 1::2]
    d = d[:, :-1] + pa * (s[:, :-1] + s[:, 1:])
    s = s[:, 1:-1] + ub * (d[:, :-1] + d[:, 1:])
    d = d[:, 1:-1] + pg * (s[:, :-1] + s[:, 1:])
    s = s[:, 1:-1] + ue * (d[:, :-1] + d[:, 1:])
    low, high = s * scaling, d[:, 1:] / scaling
    kinds = []
    for k in (0, 1, 3):
        rows = slice(WINDOW_START[k], WINDOW_START[k] + 512)
        cols = slice(128 * k, 128 * k + 128)
        kinds.append(np.concatenate([low[rows, cols], high[rows, cols]], 1))
    full = np.stack(kinds)
    head = full.astype(np.float32).astype(ml_dtypes.bfloat16)
    rest = (full - head.astype(np.float64)).astype(np.float32).astype(ml_dtypes.bfloat16)
    return np.stack([head, rest], 1)


def factor(e_ref, band):
    shift = lax.shift_left(jnp.int32(1), 15 - e_ref[band - 1]).astype(F32)
    ups = 2 - 2 * (band // 4) - 2 * ((band // 2) % 2)
    return shift * (2.0**-15 * scaling**ups)


def x_lift_quarter(cells, rims, e_ref, c, by, bz, put, low_put):
    half = ROWS // 2
    low_band, high_band = 2 * by + bz, 4 + 2 * by + bz
    high_scale = factor(e_ref, high_band)
    low_scale = factor(e_ref, low_band) if low_band else None

    def body(at, carry):
        k, t = at // 4, lax.rem(at, 4)
        j = 4 * bz + k
        row = pl.multiple_of(half * by + 8 * t, 8)

        def plane(p):
            return cells[j, pl.ds(pl.multiple_of(p * ROWS + row, 8), 8), :]

        s = [plane(2 * i) for i in range(8)]
        d = [plane(2 * i + 1) for i in range(8)]
        pv = rims[0, c, 0, j, pl.ds(row, 8), :]
        qv = rims[0, c, 1, j, pl.ds(row, 8), :]
        sv = rims[1, c, 0, j, pl.ds(row, 8), :]
        dv = rims[1, c, 1, j, pl.ds(row, 8), :]
        s.append(sv)
        d = [d[i] + pa * (s[i] + s[i + 1]) for i in range(8)]
        dm = pv + pa * s[0]
        sn = sv + ub * (d[7] + dv)
        sm = qv + ub * dm
        s = [s[i] + ub * ((d[i - 1] if i else dm) + d[i]) for i in range(8)]
        dm = dm + pg * (sm + s[0])
        s.append(sn)
        d = [d[i] + pg * (s[i] + s[i + 1]) for i in range(8)]
        s = [s[i] + ue * ((d[i - 1] if i else dm) + d[i]) for i in range(8)]
        lanes = pl.ds(pl.multiple_of(128 * k, 128), 128)
        rows = pl.ds(pl.multiple_of(8 * t, 8), 8)
        for i in range(8):
            v = d[i] * high_scale
            put(high_band, i, rows, lanes, v - jnp.clip(v, -0.5, 0.5))
            if low_band:
                v = s[i] * low_scale
                put(low_band, i, rows, lanes, v - jnp.clip(v, -0.5, 0.5))
            else:
                low_put(k, t, i, s[i] * (scaling * scaling))
        return carry

    lax.fori_loop(0, 16, body, 0)


def turn_blocks(received, c, put):
    def body(g, carry):
        put(pl.ds(pl.multiple_of(128 * g, 128), 128), received[c, g].reshape((128, 128)).T)
        return carry

    lax.fori_loop(0, 8, body, 0)


def kernel(
    n_narrow, n_wide,
    x_ref, e_ref, w_ref, ap_ref, det_ref, a_last, xr, lrecv,
    a_first, a_second, b_buf, hl, wv, ys, yr, yz, xs, ms, mr, lll, lsend, lmid,
    load_sem, outer_sem, w_sem, y_send, y_recv, x_send, x_recv, m_send, m_recv, l_send, l_recv,
):
    cells = (a_first, a_second, a_last)
    nar = lax.axis_index("narrow")
    wid = lax.axis_index("wide")
    up = lax.rem(nar + n_narrow - 1, n_narrow)
    down = lax.rem(nar + 1, n_narrow)
    left = lax.rem(wid + n_wide - 1, n_wide)
    right = lax.rem(wid + 1, n_wide)
    has_up, has_down = nar > 0, nar < n_narrow - 1
    has_left, has_right = wid > 0, wid < n_wide - 1

    def load(c, j):
        return pltpu.make_async_copy(
            x_ref.at[c, :, pl.ds(128 * j, 128)], cells[c].at[j], load_sem.at[c, j]
        )

    def load_outer(side, j):
        rows = pl.ds(3 * TILE * side, TILE)
        return pltpu.make_async_copy(
            x_ref.at[0, rows, pl.ds(128 * j, 128)], cells[0].at[j, rows], outer_sem.at[side, j]
        )

    def load_inner(j):
        rows = pl.ds(TILE, 2 * TILE)
        return pltpu.make_async_copy(
            x_ref.at[0, rows, pl.ds(128 * j, 128)], cells[0].at[j, rows], load_sem.at[0, j]
        )

    load_w = pltpu.make_async_copy(w_ref, wv, w_sem)
    for j in range(CHUNKS):
        load_outer(0, j).start()
        load_outer(1, j).start()

    barrier = pltpu.get_barrier_semaphore()

    def greet(off, carry):
        for peer in (
            4 * lax.rem(wid // 4 + off, 4) + lax.rem(wid, 4),
            4 * (wid // 4) + lax.rem(wid + off, 4),
        ):
            pl.semaphore_signal(barrier, inc=1, device_id={"wide": peer}, device_id_type=MESH)
        return carry

    lax.fori_loop(1, 4, greet, 0)
    turn_left = jnp.logical_and(lax.rem(wid, 4) == 0, has_left)
    turn_right = jnp.logical_and(lax.rem(wid, 4) == 3, has_right)

    @pl.when(turn_left)
    def _():
        pl.semaphore_signal(barrier, inc=1, device_id={"wide": left}, device_id_type=MESH)

    @pl.when(turn_right)
    def _():
        pl.semaphore_signal(barrier, inc=1, device_id={"wide": right}, device_id_type=MESH)

    @pl.when(has_up)
    def _():
        pl.semaphore_signal(barrier, inc=1, device_id={"narrow": up}, device_id_type=MESH)

    @pl.when(has_down)
    def _():
        pl.semaphore_signal(barrier, inc=1, device_id={"narrow": down}, device_id_type=MESH)

    for j in range(CHUNKS):
        load_inner(j).start()

    def y_copy(side, c):
        return pltpu.make_async_remote_copy(
            src_ref=ys.at[side, c],
            dst_ref=yr.at[1 - side, c],
            send_sem=y_send.at[side, c],
            recv_sem=y_recv.at[1 - side, c],
            device_id={"narrow": up if side == 0 else down},
            device_id_type=MESH,
        )

    def loaded(c):
        for j in range(CHUNKS):
            (load(c, j) if c else load_inner(j)).wait()
        if c + 1 < COMPS:
            for j in range(CHUNKS):
                load(c + 1, j).start()

    def y_values(c):
        def body(j, carry):
            def row(r):
                return cells[c][j, pl.ds(r, PLANES, stride=ROWS), :]

            r0, r1, r2 = row(0), row(1), row(2)
            e0, e1, e2, e3 = row(ROWS - 4), row(ROWS - 3), row(ROWS - 2), row(ROWS - 1)
            before_last = e1 + pa * (e0 + e2)
            ys[0, c, j, 0:PLANES, :] = r0
            ys[0, c, j, PLANES:, :] = r1 + pa * (r0 + r2)
            ys[1, c, j, 0:PLANES, :] = e3 + pa * e2
            ys[1, c, j, PLANES:, :] = e2 + ub * before_last

            @pl.when(jnp.logical_not(has_up))
            def _():
                r3, r4 = row(3), row(4)
                yr[0, c, j, 0:PLANES, :] = r1 + pa * r2
                yr[0, c, j, PLANES:, :] = r2 + ub * (r3 + pa * (r2 + r4))

            @pl.when(jnp.logical_not(has_down))
            def _():
                yr[1, c, j, 0:PLANES, :] = e2
                yr[1, c, j, PLANES:, :] = before_last

            return carry

        lax.fori_loop(0, CHUNKS, body, 0)

        @pl.when(has_up)
        def _():
            y_copy(0, c).start()

        @pl.when(has_down)
        def _():
            y_copy(1, c).start()

    def z_rows(m, get, put):
        for j in range(CHUNKS):
            value = get(j)
            head = value.astype(BF16)
            hl[0:m, 128 * j : 128 * j + 128] = head
            hl[m : 2 * m, 128 * j : 128 * j + 128] = (value - head.astype(F32)).astype(BF16)
        for k in range(CHUNKS // 2):
            start, kind = WINDOW_START[k], WINDOW_KIND[k]
            both = jnp.dot(
                hl[0 : 2 * m, start : start + 512], wv[kind, 0], preferred_element_type=F32
            )
            rest = jnp.dot(hl[0:m, start : start + 512], wv[kind, 1], preferred_element_type=F32)
            out = both[:m] + (both[m:] + rest)
            put(k, out[:, :128])
            put(CHUNKS // 2 + k, out[:, 128:])

    def z_tiles(c, first, step, count=2):
        def body(t, carry):
            base = pl.multiple_of((first + step * t) * TILE, TILE)

            def put(j, value):
                b_buf[c, j, pl.ds(base, TILE), :] = value

            z_rows(TILE, lambda j: cells[c][j, pl.ds(base, TILE), :], put)
            return carry

        lax.fori_loop(0, count, body, 0)

    def y_arrived(c):
        @pl.when(has_up)
        def _():
            y_copy(1, c).wait_recv()

        @pl.when(has_down)
        def _():
            y_copy(0, c).wait_recv()

    def z_halo(c):
        def put(j, value):
            yz[c, j] = value

        z_rows(
            4 * PLANES,
            lambda j: jnp.concatenate([yr[0, c, j], yr[1, c, j]], 0),
            put,
        )

    half = ROWS // 2
    row_at = lax.broadcasted_iota(jnp.int32, (half, 128), 0)

    def following(value, last):
        return jnp.where(row_at == half - 1, last, pltpu.roll(value, half - 1, 0))

    def preceding(value, first):
        return jnp.where(row_at == 0, first, pltpu.roll(value, 1, 0))

    def y_plane(c, p, j):
        base = pl.multiple_of(p * ROWS, ROWS)
        s, d = y_rows(c, j, base, [yz[c, j, pl.ds(PLANES * kind + p, 1), :] for kind in range(4)])
        cells[c][j, pl.ds(base, half), :] = s
        cells[c][j, pl.ds(base + half, half), :] = d

    def y_rows(c, j, base, rim):
        s = b_buf[c, j, pl.ds(base, half, stride=2), :]
        d = b_buf[c, j, pl.ds(base + 1, half, stride=2), :]
        pv, qv, sv, dv = rim
        d = d + pa * (s + following(s, sv))
        dm = pv + pa * s[0:1]
        s = s + ub * (preceding(d, dm) + d)
        sn = sv + ub * (d[half - 1 :] + dv)
        sm = qv + ub * dm
        dm = dm + pg * (sm + s[0:1])
        d = d + pg * (s + following(s, sn))
        s = s + ue * (preceding(d, dm) + d)
        return s, d

    def y_planes(c, starts):
        for start in starts:
            def body(q, carry):
                for j in range(CHUNKS):
                    y_plane(c, start + q, j)
                return carry

            lax.fori_loop(0, 4, body, 0)

    parts = ((0, 4, 0, half), (4, 4, 0, half), (0, 8, half, half), (0, 8, 0, ROWS))

    def x_copy(side, c, part):
        j0, jn, r0, rn = parts[part]
        place = (c, slice(None), pl.ds(j0, jn), pl.ds(r0, rn), slice(None))
        return pltpu.make_async_remote_copy(
            src_ref=xs.at[(side, *place)],
            dst_ref=xr.at[(1 - side, *place)],
            send_sem=x_send.at[side, c, part],
            recv_sem=x_recv.at[1 - side, c, part],
            device_id={"wide": left if side == 0 else right},
            device_id_type=MESH,
        )

    def x_values(c):
        def body(j, carry):
            def plane(p):
                return cells[c][j, p * ROWS : p * ROWS + ROWS, :]

            p0 = plane(0)
            xs[0, c, 0, j] = p0
            xs[0, c, 1, j] = plane(1) + pa * (p0 + plane(2))
            e2 = plane(PLANES - 2)
            xs[1, c, 0, j] = plane(PLANES - 1) + pa * e2
            xs[1, c, 1, j] = e2 + ub * (plane(PLANES - 3) + pa * (plane(PLANES - 4) + e2))
            return carry

        lax.fori_loop(0, CHUNKS, body, 0)

    def x_ends(c):
        def body(j, carry):

            def plane(p):
                return cells[c][j, p * ROWS : p * ROWS + ROWS, :]

            @pl.when(jnp.logical_not(has_left))
            def _():
                xr[0, c, 0, j] = plane(1) + pa * plane(2)
                xr[0, c, 1, j] = plane(2) + ub * (plane(3) + pa * (plane(2) + plane(4)))

            @pl.when(jnp.logical_not(has_right))
            def _():
                xr[1, c, 0, j] = plane(PLANES - 2)
                xr[1, c, 1, j] = plane(PLANES - 3) + pa * (plane(PLANES - 4) + plane(PLANES - 2))

            return carry

        lax.fori_loop(0, CHUNKS, body, 0)

    def x_start(c, part):
        @pl.when(has_left)
        def _():
            x_copy(0, c, part).start()

        @pl.when(has_right)
        def _():
            x_copy(1, c, part).start()

    def x_arrived(c, part):
        @pl.when(has_left)
        def _():
            x_copy(1, c, part).wait_recv()

        @pl.when(has_right)
        def _():
            x_copy(0, c, part).wait_recv()

    def m_copy(side):
        return pltpu.make_async_remote_copy(
            src_ref=ms.at[side],
            dst_ref=mr.at[1 - side],
            send_sem=m_send.at[side],
            recv_sem=m_recv.at[1 - side],
            device_id={"wide": left if side == 0 else right},
            device_id_type=MESH,
        )

    def m_values():
        def body(j, carry):
            for kind in range(4):
                def row(p):
                    return yr[kind // 2, 0, j, pl.ds(PLANES * (kind % 2) + p, 1), :]

                e2 = row(PLANES - 2)
                ms[0, j, kind : kind + 1, :] = row(0)
                ms[0, j, 4 + kind : 5 + kind, :] = row(1) + pa * (row(0) + row(2))
                ms[1, j, kind : kind + 1, :] = row(PLANES - 1) + pa * e2
                ms[1, j, 4 + kind : 5 + kind, :] = e2 + ub * (
                    row(PLANES - 3) + pa * (row(PLANES - 4) + e2)
                )
            return carry

        lax.fori_loop(0, CHUNKS, body, 0)

        @pl.when(has_left)
        def _():
            m_copy(0).start()

        @pl.when(has_right)
        def _():
            m_copy(1).start()

    def m_lift():
        x_arrived(0, 3)

        @pl.when(has_left)
        def _():
            m_copy(1).wait_recv()

        @pl.when(has_right)
        def _():
            m_copy(0).wait_recv()

        def get(j):
            return jnp.concatenate(
                [xr[0, 0, 0, j], xr[0, 0, 1, j], xr[1, 0, 0, j], xr[1, 0, 1, j], mr[0, j], mr[1, j]], 0
            )

        def put(j, value):
            b_buf[0, j, 0 : TILE + 16, :] = value

        z_rows(TILE + 16, get, put)

        def side_lift(side):
            def body(j, carry):
                for combo in range(2):
                    at = TILE + 8 * side + 4 * combo
                    s, d = y_rows(
                        0, j, ROWS * (2 * side + combo),
                        [b_buf[0, j, at + kind : at + kind + 1, :] for kind in range(4)],
                    )
                    xr[side, 0, combo, j, 0:half, :] = s
                    xr[side, 0, combo, j, half:, :] = d
                return carry

            lax.fori_loop(0, CHUNKS, body, 0)

        @pl.when(has_left)
        def _():
            side_lift(0)

        @pl.when(has_right)
        def _():
            side_lift(1)

    def x_lift(c, by, bz):
        def low_put(k, t, i, value):
            lll[k, pl.ds(pl.multiple_of(half * i + 8 * t, 8), 8), :] = value

        def put(band, i, rows, lanes, value):
            det_ref[c, band - 1, i, rows, lanes] = value

        x_lift_quarter(cells[c], xr, e_ref, c, by, bz, put, low_put)

    lane = lax.broadcasted_iota(jnp.int32, (8, 128), 1)
    low_half = lane < 64
    low_quarter = lax.rem(lane, 64) < 32

    xpos, zpos = wid // 4, lax.rem(wid, 4)

    def across(c, off, source):
        peer = lax.rem(xpos + off, 4)
        return pltpu.make_async_remote_copy(
            src_ref=lsend.at[pl.ds(4 * peer, 4), c],
            dst_ref=lmid.at[c, :, :, source],
            send_sem=l_send.at[0, c, off - 1],
            recv_sem=l_recv.at[0, c, source],
            device_id={"wide": 4 * peer + zpos},
            device_id_type=MESH,
        )

    def along(c, off, source):
        peer = lax.rem(zpos + off, 4)
        return pltpu.make_async_remote_copy(
            src_ref=lmid.at[c, peer],
            dst_ref=lrecv.at[c, :, :, source],
            send_sem=l_send.at[1, c, off - 1],
            recv_sem=l_recv.at[1, c, source],
            device_id={"wide": 4 * xpos + peer},
            device_id_type=MESH,
        )

    def l_pack(c):
        def body(k, carry):
            for g in range(8):
                v = [lll[k, pl.ds(4 * g + y, 8, stride=half), :] for y in range(4)]
                for a, b in ((0, 2), (1, 3)):
                    v[a], v[b] = (
                        jnp.where(low_half, v[a], pltpu.roll(v[b], 64, 1)),
                        jnp.where(low_half, pltpu.roll(v[a], 64, 1), v[b]),
                    )
                for a, b in ((0, 1), (2, 3)):
                    v[a], v[b] = (
                        jnp.where(low_quarter, v[a], pltpu.roll(v[b], 32, 1)),
                        jnp.where(low_quarter, pltpu.roll(v[a], 96, 1), v[b]),
                    )
                for y in range(4):
                    lsend[4 * k + y, c, g] = v[y]
            return carry

        lax.fori_loop(0, 4, body, 0)

        for off in (2, 1, 3):
            across(c, off, xpos).start()

        def own(z, carry):
            lmid[c, z, :, xpos] = lsend[4 * xpos + z, c]
            return carry

        lax.fori_loop(0, 4, own, 0)

    def l_turn(c):
        for off in (2, 1, 3):
            across(c, off, lax.rem(xpos + off, 4)).wait_recv()
        for off in (2, 1, 3):
            along(c, off, zpos).start()
        lrecv[c, :, :, zpos] = lmid[c, zpos]

    def l_arrived(c):
        for off in (2, 1, 3):
            along(c, off, lax.rem(zpos + off, 4)).wait_recv()

    def l_take(c):
        l_arrived(c)

        def put(rows, value):
            ap_ref[c, rows, :] = value

        turn_blocks(lrecv, c, put)

    for j in range(CHUNKS):
        load_outer(0, j).wait()
        load_outer(1, j).wait()
    x_values(0)
    pl.semaphore_wait(
        barrier,
        6
        + turn_left.astype(jnp.int32)
        + turn_right.astype(jnp.int32)
        + has_up.astype(jnp.int32)
        + has_down.astype(jnp.int32),
    )
    x_start(0, 3)
    loaded(0)
    load_w.start()
    loaded(1)
    y_values(1)
    y_values(0)
    load_w.wait()
    z_tiles(1, 0, 3)
    loaded(2)
    y_values(2)
    y_arrived(1)
    z_halo(1)
    y_planes(1, (0, 12))
    x_values(1)
    x_start(1, 0)
    x_start(1, 1)
    y_arrived(0)
    m_values()
    z_tiles(2, 0, 3)
    y_arrived(2)
    z_halo(2)
    y_planes(2, (0, 12))
    x_values(2)
    x_start(2, 0)
    x_start(2, 1)
    z_tiles(0, 0, 1, 4)
    z_halo(0)
    y_planes(0, (0, 4, 8, 12))
    m_lift()
    x_ends(0)
    x_lift(0, 0, 0)
    l_pack(0)
    x_start(1, 2)
    x_lift(0, 0, 1)
    z_tiles(1, 1, 1)
    y_planes(1, (4, 8))
    l_turn(0)
    x_ends(1)
    x_arrived(1, 0)
    x_lift(1, 0, 0)
    l_pack(1)
    z_tiles(2, 1, 1)
    y_planes(2, (4, 8))
    l_turn(1)
    x_start(2, 2)
    x_ends(2)
    x_arrived(2, 0)
    x_lift(2, 0, 0)
    l_pack(2)
    x_lift(0, 1, 0)
    l_turn(2)
    x_lift(0, 1, 1)
    for c in (1, 2):
        x_arrived(c, 1)
        x_lift(c, 0, 1)
    x_arrived(1, 2)
    x_lift(1, 1, 0)
    x_lift(1, 1, 1)
    l_take(0)
    l_take(1)
    x_arrived(2, 2)
    l_arrived(2)

    for c in range(COMPS):
        @pl.when(has_up)
        def _():
            y_copy(0, c).wait_send()

        @pl.when(has_down)
        def _():
            y_copy(1, c).wait_send()

        for part in (range(3) if c else (3,)):
            @pl.when(has_left)
            def _():
                x_copy(0, c, part).wait_send()

            @pl.when(has_right)
            def _():
                x_copy(1, c, part).wait_send()

        if c == 0:
            @pl.when(has_left)
            def _():
                m_copy(0).wait_send()

            @pl.when(has_right)
            def _():
                m_copy(1).wait_send()

        for off in (1, 2, 3):
            across(c, off, xpos).wait_send()
            along(c, off, zpos).wait_send()


def finish(
    e_ref, cells, rims, received, approx, details, approx_out, details_out,
    last_details, last_approx, approx_sem, details_sem,
):
    c = COMPS - 1
    bands = (2, 3, 6, 7)
    early, late = [], {}
    for comp in range(COMPS):
        for band in range(1, 8):
            mine = comp == c and band in bands
            source = last_details.at[bands.index(band)] if mine else details.at[comp, band - 1]
            copy = pltpu.make_async_copy(
                source, details_out.at[comp, band - 1], details_sem.at[comp, band - 1]
            )
            if mine:
                late[band] = copy
            else:
                early.append(copy)
        copy = pltpu.make_async_copy(
            last_approx if comp == c else approx.at[comp], approx_out.at[comp], approx_sem.at[comp]
        )
        if comp == c:
            late[0] = copy
        else:
            early.append(copy)
    for copy in early:
        copy.start()

    def put(band, i, rows, lanes, value):
        last_details[bands.index(band), i, rows, lanes] = value

    for bz in range(2):
        x_lift_quarter(cells, rims, e_ref, c, 1, bz, put, None)
        late[2 + bz].start()
        late[6 + bz].start()

    def put_block(rows, value):
        last_approx[rows, :] = value

    turn_blocks(received, c, put_block)
    late[0].start()
    for copy in early + list(late.values()):
        copy.wait()


def local(n_narrow, n_wide, velocity, exponents):
    cells = velocity.reshape((COMPS, PLANES * ROWS, DEPTH))
    approx, details, last, rims, received = pl.pallas_call(
        functools.partial(kernel, n_narrow, n_wide),
        out_shape=(
            pltpu.VMEM((COMPS - 1, 1024, 128), F32),
            pltpu.VMEM((COMPS, 7, PLANES // 2, ROWS // 2, DEPTH // 2), F32),
            pltpu.VMEM((CHUNKS, PLANES * ROWS, 128), F32),
            pltpu.VMEM((2, COMPS, 2, CHUNKS, ROWS, 128), F32),
            pltpu.VMEM((COMPS, 8, 4, 4, 8, 128), F32),
        ),
        in_specs=[
            pl.BlockSpec(memory_space=pl.ANY),
            pl.BlockSpec(memory_space=pltpu.SMEM),
            pl.BlockSpec(memory_space=pl.ANY),
        ],
        out_specs=(pl.BlockSpec(memory_space=pltpu.VMEM),) * 5,
        scratch_shapes=[
            pltpu.VMEM((CHUNKS, PLANES * ROWS, 128), F32),
            pltpu.VMEM((CHUNKS, PLANES * ROWS, 128), F32),
            pltpu.VMEM((COMPS, CHUNKS, PLANES * ROWS, 128), F32),
            pltpu.VMEM((2 * TILE + 32, DEPTH), BF16),
            pltpu.VMEM((3, 2, 512, 256), BF16),
            pltpu.VMEM((2, COMPS, CHUNKS, 2 * PLANES, 128), F32),
            pltpu.VMEM((2, COMPS, CHUNKS, 2 * PLANES, 128), F32),
            pltpu.VMEM((COMPS, CHUNKS, 4 * PLANES, 128), F32),
            pltpu.VMEM((2, COMPS, 2, CHUNKS, ROWS, 128), F32),
            pltpu.VMEM((2, CHUNKS, 8, 128), F32),
            pltpu.VMEM((2, CHUNKS, 8, 128), F32),
            pltpu.VMEM((4, 256, 128), F32),
            pltpu.VMEM((16, COMPS, 8, 8, 128), F32),
            pltpu.VMEM((COMPS, 4, 8, 4, 8, 128), F32),
            pltpu.SemaphoreType.DMA((COMPS, CHUNKS)),
            pltpu.SemaphoreType.DMA((2, CHUNKS)),
            pltpu.SemaphoreType.DMA,
            pltpu.SemaphoreType.DMA((2, COMPS)),
            pltpu.SemaphoreType.DMA((2, COMPS)),
            pltpu.SemaphoreType.DMA((2, COMPS, 4)),
            pltpu.SemaphoreType.DMA((2, COMPS, 4)),
            pltpu.SemaphoreType.DMA((2,)),
            pltpu.SemaphoreType.DMA((2,)),
            pltpu.SemaphoreType.DMA((2, COMPS, 3)),
            pltpu.SemaphoreType.DMA((2, COMPS, 4)),
        ],
        compiler_params=pltpu.CompilerParams(
            collective_id=0, has_side_effects=True, vmem_limit_bytes=38 * 1024 * 1024
        ),
        cost_estimate=pl.CostEstimate(
            flops=10_000_000_000, bytes_accessed=26_000_000, transcendentals=0
        ),
    )(cells, exponents, jnp.asarray(z_weights()))
    approx, details = pl.pallas_call(
        finish,
        out_shape=(
            jax.ShapeDtypeStruct((COMPS, 1024, 128), F32),
            jax.ShapeDtypeStruct(details.shape, F32),
        ),
        in_specs=[pl.BlockSpec(memory_space=pltpu.SMEM)]
        + [pl.BlockSpec(memory_space=pltpu.VMEM)] * 3
        + [pl.BlockSpec(memory_space=pl.ANY)] * 2,
        out_specs=(pl.BlockSpec(memory_space=pl.ANY),) * 2,
        scratch_shapes=[
            pltpu.VMEM((4, PLANES // 2, ROWS // 2, DEPTH // 2), F32),
            pltpu.VMEM((1024, 128), F32),
            pltpu.SemaphoreType.DMA((COMPS,)),
            pltpu.SemaphoreType.DMA((COMPS, 7)),
        ],
        compiler_params=pltpu.CompilerParams(vmem_limit_bytes=4 * 1024 * 1024),
    )(exponents, last, rims, received, approx, details)
    approx = approx.reshape((COMPS, ROWS // 2, 32, 128))
    return jnp.transpose(approx, (0, 3, 1, 2)), details


def solution(mesh):
    placed = (P(None, "wide", "narrow", None), P())
    return jax.shard_map(
        functools.partial(local, mesh.shape["narrow"], mesh.shape["wide"]),
        mesh=mesh,
        in_specs=placed,
        out_specs=(P(None, None, "narrow", "wide"), P(None, None, "wide", "narrow", None)),
        check_vma=False,
    )
```
